512 devices in a mesh: queue: 16 (over x, y_hi, core), seq: 32 (over z, y_lo).
Axes of the slice: x: 4, y: 4 (y_hi: 2, y_lo: 2; y = y_hi * 2 + y_lo), z: 16, core: 2. Of those that a mesh axis runs over, the one named last changes fastest.
Arguments:
- projected: bfloat16 [3, 24576, 4096], P(None, ('queue', 'seq')), may hold values from -8 to 8
- out_weight: bfloat16 [5120, 4096], P('seq'), may hold values from -2 to 2
- head_weight: bfloat16 [5120, 64], P('seq'), may hold values from -0.078125 to 0.078125
- hidden_in: bfloat16 [5120, 24576], P('seq', 'queue'), may hold values from -30 to 30
- latent: float32 [24576, 64], P(('queue', 'seq')), may hold values from -6 to 6
- fresh_noise: float32 [1536, 64], P('seq'), may hold values from -6 to 6
- levels: int32 [16], P('queue'), may hold values from 0 to 49
Outputs:
- block_out: float32 [5120, 24576], P('seq', 'queue')
- velocity: float32 [24576, 64], P(('queue', 'seq'))
- queue_next: float32 [24576, 64], P(('queue', 'seq'))
The draws below stay inside these ranges and needn't reach their ends.
All inputs are finite; a program needn't handle non-finite values.
Results may differ from the reference program's by a relative error of at most 0.0042.
Values may be sent and summed in bfloat16 or wider, within the bound.
A program may use at most 64 MiB of HBM per device.

```python
import math
import jax
import jax.numpy as jnp
from jax import lax

DOUT = 5120
H = 32
HD = 128
PC = 64
STEPS = 50
SEQ = 1536
TOKENS = 24576
N_QUEUE = 16


def draw_projected(key, part):
    key = jax.random.fold_in(key, 11)
    first = jax.random.fold_in(key, 0)
    shape = (3, TOKENS, H * HD)
    base = jax.random.truncated_normal(first, -6.0, 6.0, shape, jnp.float32)
    return base.astype(jnp.bfloat16)


def draw_hidden_in(key, part):
    key = jax.random.fold_in(key, 5)
    first, second = jax.random.split(key)
    feature = jnp.arange(DOUT, dtype=jnp.float32) / DOUT
    base = jax.random.truncated_normal(first, -6.0, 6.0, (DOUT, TOKENS), jnp.float32)
    rise = 3.0 ** feature
    factor = jax.random.uniform(second, (DOUT,), jnp.float32, 0.7, 1.4)
    return (base * (rise * factor)[:, None]).astype(jnp.bfloat16)


def touch_ends(values, own_key, least, high):
    longest = values.shape.index(max(values.shape))
    spots = []
    for shift in (0, 1):
        where = [jax.random.randint(jax.random.fold_in(own_key, axis), (), 0, length) for axis, length in enumerate(values.shape)]
        where[longest] = (where[longest] + shift) % values.shape[longest]
        spots.append(tuple(where))
    return values.at[spots[0]].set(least).at[spots[1]].set(high)


def shard_levels(key, extent, shards, least, largest):
    loudness, own = 1.0, jax.random.fold_in(key, 6)
    for axis_at, shards_of in shards:
        heights = jnp.exp(jax.random.uniform(jax.random.fold_in(own, axis_at), (shards_of,), jnp.float32, least / len(shards), largest / len(shards)))
        loudness = loudness * jnp.repeat(heights, extent[axis_at] // shards_of).reshape([-1 if axis == axis_at else 1 for axis in range(len(extent))])
    return loudness


def noise(rng, dims, deviation, limit, cuts=(), held_as=jnp.bfloat16):
    values = deviation * jax.random.normal(rng, dims, jnp.float32)
    if cuts:
        values = values * shard_levels(rng, dims, cuts, -0.22, 0.18)
    return jnp.clip(values, -limit, limit).astype(held_as)


def setup_inputs(seed: int = 0) -> dict:
    arg_keys = jax.random.split(jax.random.key(seed), 8)
    return {
        "projected": draw_projected(jax.random.fold_in(arg_keys[7], 71), 0),
        "out_weight": noise(arg_keys[1], (DOUT, H * HD), (max(1, 3 * H * HD // SEQ)) ** -0.5, 2.0, ((0, 32),)),
        "head_weight": noise(arg_keys[2], (DOUT, PC), DOUT ** -0.5, 0.078125, ((0, 32),)),
        "hidden_in": draw_hidden_in(jax.random.fold_in(arg_keys[7], 71), 0),
        "latent": noise(arg_keys[4], (TOKENS, PC), 1.0, 6.0, ((0, 512),), jnp.float32),
        "fresh_noise": noise(arg_keys[5], (SEQ, PC), 1.0, 6.0, ((0, 32),), jnp.float32),
        "levels": touch_ends(jax.random.randint(arg_keys[6], (N_QUEUE,), 0, STEPS), jax.random.fold_in(arg_keys[6], 1), 0, STEPS - 1).astype(jnp.int32),
    }


def attend(queries, keys, values):
    length = queries.shape[0]
    block = math.gcd(length, 512)
    grouped = queries.reshape(length // block, block, queries.shape[1])

    def one_block(query_block):
        scores = lax.dot_general(query_block, keys, (((1,), (1,)), ((), ())), preferred_element_type=jnp.float32)
        scores = scores * queries.shape[1] ** (-0.5)
        peak = lax.optimization_barrier(jnp.max(scores, axis=1, keepdims=True))
        raw = jnp.exp(scores - peak)
        total = lax.optimization_barrier(jnp.sum(raw, axis=1, keepdims=True))
        probs = raw.astype(jnp.bfloat16)
        mixed = jnp.dot(probs, values, preferred_element_type=jnp.float32) / total
        return mixed.astype(jnp.bfloat16)
    return lax.map(one_block, grouped).reshape(length, queries.shape[1])

def sigma_of(level):
    frac = 1.0 - level / STEPS
    return 5.0 * frac / (1.0 + 4.0 * frac)

def reference(projected, out_weight, head_weight, hidden_in, latent, fresh_noise, levels):

    def one_group(group):
        slab = lax.dynamic_slice_in_dim(projected, group * SEQ, SEQ, 1)
        head_view = slab.reshape(3, SEQ, H, HD)

        def one_head(head):
            picked = lax.dynamic_index_in_dim(head_view, head, 2, keepdims=False)
            return attend(picked[0], picked[1], picked[2])
        results = lax.map(one_head, jnp.arange(H, dtype=jnp.int32))
        attended = jnp.transpose(results, (1, 0, 2)).reshape(SEQ, H * HD)
        update = lax.dot_general(attended, out_weight, (((1,), (1,)), ((), ())), preferred_element_type=jnp.float32)
        rows_in = lax.dynamic_slice_in_dim(hidden_in, group * SEQ, SEQ, 1).astype(jnp.float32)
        return jnp.transpose(rows_in) + update
    block_rows = lax.map(one_group, jnp.arange(N_QUEUE, dtype=jnp.int32)).reshape(TOKENS, DOUT)
    scale = lax.rsqrt(lax.optimization_barrier(jnp.mean(block_rows * block_rows, axis=1, keepdims=True)) + 1e-06)
    normed = (block_rows * scale).astype(jnp.bfloat16)
    velocity = jnp.dot(normed, head_weight, preferred_element_type=jnp.float32)
    level_now = levels.astype(jnp.float32)
    delta = sigma_of(level_now + 1.0) - sigma_of(level_now)
    stepped = latent + jnp.repeat(delta, SEQ)[:, None] * velocity
    queue_next = jnp.concatenate([fresh_noise, stepped[:TOKENS - SEQ]], axis=0)
    return (jnp.transpose(block_rows), velocity, queue_next)
```

```python
import functools
import math

import jax
import jax.numpy as jnp
from jax import lax
from jax.experimental import pallas as pl
from jax.experimental.pallas import tpu as pltpu
from jax.sharding import PartitionSpec as P

MESH = pl.DeviceIdType.MESH
F32 = jnp.float32
BF16 = jnp.bfloat16
STEPS = 50
SKEW = 2
LOG2E = 1.4426950408889634


def contract_last(a, b):
    return lax.dot_general(a, b, (((1,), (1,)), ((), ())), preferred_element_type=F32)


def sigma_of(level):
    frac = 1.0 - level / STEPS
    return 5.0 * frac / (1.0 + 4.0 * frac)


def split_squares(vel, squares):
    lane = lax.broadcasted_iota(jnp.int32, vel.shape, 1)
    high = squares.astype(BF16).astype(F32)
    rest = squares - high
    middle = rest.astype(BF16).astype(F32)
    low = rest - middle
    tail = jnp.where(lane == 64, high, jnp.where(lane == 65, middle, jnp.where(lane == 66, low, 0.0)))
    return jnp.where(lane < 64, vel, tail).astype(BF16)


def sum_squares_lanes(total):
    lane = lax.broadcasted_iota(jnp.int32, total.shape, 1)
    return jnp.sum(jnp.where(lane >= 64, total, 0.0), axis=1, keepdims=True)


def kernel(
    n_queue, n_z, n_chunks, d_out,
    proj_hbm, w_hbm, hw_ref, hid_ref, lat_ref, fresh_ref, lev_ref,
    out_ref, vel_ref, next_ref,
    projv, qkv, vt, scores, att, wbuf, acc, hwp, rs_send, rs_recv, pay, y_recv, z_send, z_recv, n_send, n_recv,
    proj_sem, own_sem, kv_send, kv_recv, q_send, q_recv, w_own, w_send, w_recv,
    ag_send, ag_recv, rs_ssem, rs_rsem, y_ssem, y_rsem, z_ssem, z_rsem, n_ssem, n_rsem,
):
    n_seq = 2 * n_z
    half = n_z // 2
    tok = proj_hbm.shape[1]
    hd = qkv.shape[2]
    n_tok = qkv.shape[1]
    chunk = n_tok // n_chunks
    own_z = n_z // n_chunks
    rows = w_hbm.shape[0]
    group = lax.axis_index("queue")
    me = lax.axis_index("seq")
    z = me // 2
    y = me % 2
    partner = 2 * z + (1 - y)
    after = (group + 1) % n_queue
    before = (group + n_queue - 1) % n_queue

    load = pltpu.make_async_copy(proj_hbm, projv, proj_sem)
    load.start()

    @pl.loop(0, n_z)
    def _(i):
        pltpu.make_async_copy(
            w_hbm.at[:, pl.ds(pl.multiple_of((2 * i + y) * hd, hd), hd)], wbuf.at[i, pl.ds(0, rows)], w_own
        ).start()

    barrier = pltpu.get_barrier_semaphore()

    @pl.loop(1, n_seq)
    def _(i):
        pl.semaphore_signal(barrier, inc=1, device_id=(group, (me + i) % n_seq), device_id_type=MESH)

    pl.semaphore_signal(barrier, inc=1, device_id=(after, me), device_id_type=MESH)
    pl.semaphore_signal(barrier, inc=1, device_id=(before, me), device_id_type=MESH)
    hwp[...] = jnp.zeros_like(hwp)
    hwp[:, 0:64] = hw_ref[...]
    pl.semaphore_wait(barrier, n_seq + 1)
    load.wait()

    def exchange(first, count, send_sem, recv_sem):
        def to(dest):
            pltpu.make_async_remote_copy(
                src_ref=projv.at[pl.ds(first, count), :, pl.ds(pl.multiple_of(dest * hd, hd), hd)],
                dst_ref=qkv.at[pl.ds(first, count), pl.ds(pl.multiple_of(me * tok, tok), tok), :],
                send_sem=send_sem,
                recv_sem=recv_sem,
                device_id=(group, dest),
                device_id_type=MESH,
            ).start()

        to(partner)

        @pl.loop(1, n_z)
        def _(i):
            far = (i + 1) // 2
            shift = (i % 2) * far + (1 - i % 2) * (n_z - far)
            there = (z + shift) % n_z
            to(2 * there + y)
            to(2 * there + (1 - y))

    exchange(1, 2, kv_send, kv_recv)
    exchange(0, 1, q_send, q_recv)
    own = pltpu.make_async_copy(
        projv.at[:, :, pl.ds(pl.multiple_of(me * hd, hd), hd)],
        qkv.at[:, pl.ds(pl.multiple_of(me * tok, tok), tok), :],
        own_sem,
    )
    own.start()

    @pl.loop(0, n_z)
    def _(i):
        pltpu.make_async_remote_copy(
            src_ref=w_hbm.at[:, pl.ds(pl.multiple_of((2 * i + 1 - y) * hd, hd), hd)],
            dst_ref=wbuf.at[i, pl.ds(rows, rows)],
            send_sem=w_send,
            recv_sem=w_recv,
            device_id=(group, partner),
            device_id_type=MESH,
        ).start()

    def whole(ref, sem):
        return pltpu.make_async_copy(ref, ref, sem)

    others = (n_seq - 1) * tok
    own.wait()
    whole(qkv.at[pl.ds(1, 2), pl.ds(0, others)], kv_recv).wait()
    vt[...] = qkv[2].T
    whole(qkv.at[pl.ds(0, 1), pl.ds(0, others)], q_recv).wait()
    whole(wbuf.at[:, pl.ds(0, rows)], w_own).wait()
    whole(wbuf.at[:, pl.ds(rows, rows)], w_recv).wait()

    def ring(c, step, way):
        origin = (z + n_z - (step - 1)) % n_z if way == 0 else (z + step - 1) % n_z
        there = (z + 1) % n_z if way == 0 else (z + n_z - 1) % n_z

        def made(block):
            return pltpu.make_async_remote_copy(
                src_ref=block,
                dst_ref=block,
                send_sem=ag_send.at[way, c, step],
                recv_sem=ag_recv.at[way, c, step],
                device_id=(group, 2 * there + y),
                device_id_type=MESH,
            )

        return made, origin

    def ring_full(c, step, way):
        made, origin = ring(c, step, way)
        return made(att.at[origin, c])

    def ring_half(c, step, way):
        made, origin = ring(c, step, way)
        return made(att.at[origin, c, pl.ds(way * (hd // 2), hd // 2)])

    key_block = math.gcd(256, n_tok)

    def attend(c):
        queries = qkv[0, pl.ds(pl.multiple_of(c * chunk, 16), chunk), :]
        peak = jnp.full((8, chunk), -jnp.inf, F32)
        for k in range(0, n_tok, key_block):
            part = contract_last(qkv[1, k : k + key_block, :], queries)
            scores[k : k + key_block, :] = part
            peak = jnp.maximum(peak, jnp.max(part.reshape(key_block // 8, 8, chunk), axis=0))
        peak = jnp.max(peak, axis=0, keepdims=True)
        total = jnp.zeros((8, chunk), F32)
        mixed = jnp.zeros((hd, chunk), F32)
        factor = LOG2E * hd ** (-0.5)
        for k in range(0, n_tok, key_block):
            raw = jnp.exp2((scores[k : k + key_block, :] - peak) * factor)
            total = total + jnp.sum(raw.reshape(key_block // 8, 8, chunk), axis=0)
            mixed = mixed + jnp.dot(vt[:, k : k + key_block], raw.astype(BF16), preferred_element_type=F32)
        total = jnp.sum(total, axis=0, keepdims=True)
        att[z, c] = (mixed / total).astype(BF16)

    def rs_copy(c):
        return pltpu.make_async_remote_copy(
            src_ref=rs_send.at[c],
            dst_ref=rs_recv.at[c],
            send_sem=rs_ssem.at[c],
            recv_sem=rs_rsem.at[c],
            device_id=(group, partner),
            device_id_type=MESH,
        )

    def y_copy(c):
        return pltpu.make_async_remote_copy(
            src_ref=pay.at[c, 1 - y],
            dst_ref=y_recv.at[c],
            send_sem=y_ssem.at[c],
            recv_sem=y_rsem.at[c],
            device_id=(group, partner),
            device_id_type=MESH,
        )

    def z_copy(c, i):
        return pltpu.make_async_remote_copy(
            src_ref=z_send.at[c, i],
            dst_ref=z_recv.at[z],
            send_sem=z_ssem.at[c, i],
            recv_sem=z_rsem,
            device_id=(group, 2 * (c * own_z + i) + y),
            device_id_type=MESH,
        )

    def finish_block(c):
        rs_copy(c).wait_recv()
        columns = pl.ds(pl.multiple_of(c * chunk, chunk), chunk)
        x = hid_ref[:, columns].astype(F32) + acc[c, 0:rows] + rs_recv[c].astype(F32)
        out_ref[:, columns] = x
        turned = x.T
        squares = jnp.sum(turned * turned, axis=1, keepdims=True)
        upper = turned.astype(BF16)
        lower = (turned - upper.astype(F32)).astype(BF16)
        vel = jnp.dot(upper, hwp[...], preferred_element_type=F32) + jnp.dot(lower, hwp[...], preferred_element_type=F32)
        lane = lax.broadcasted_iota(jnp.int32, vel.shape, 1)
        payload = jnp.where(lane == 64, squares, vel).reshape(own_z, 2, tok, 128)
        for i in range(own_z):
            pay[c, 0, i] = payload[i, 0]
            pay[c, 1, i] = payload[i, 1]
        y_copy(c).start()

    def share_out(c):
        y_copy(c).wait_recv()
        total = (pay[c, y] + y_recv[c]).reshape(own_z * tok, 128)
        summed = split_squares(total, sum_squares_lanes(total)).reshape(own_z, tok, 128)
        for i in range(own_z):
            z_send[c, i] = summed[i]

            @pl.when(c * own_z + i == z)
            def _():
                z_recv[z] = summed[i]

            @pl.when(c * own_z + i != z)
            def _():
                z_copy(c, i).start()

    @pl.loop(0, SKEW * (n_chunks - 1) + half + 3)
    def _(slot):
        @pl.loop(0, n_chunks)
        def _(c):
            step = slot - SKEW * c

            @pl.when(step == 0)
            def _():
                attend(c)
                ring_full(c, 1, 0).start()
                ring_full(c, 1, 1).start()
                acc[c] = jnp.dot(wbuf[z], att[z, c], preferred_element_type=F32)

            @pl.when(jnp.logical_and(step >= 1, step < half))
            def _():
                ring_full(c, step, 0).wait_recv()
                ring_full(c, step, 1).wait_recv()

                @pl.when(step < half - 1)
                def _():
                    ring_full(c, step + 1, 0).start()
                    ring_full(c, step + 1, 1).start()

                @pl.when(step == half - 1)
                def _():
                    ring_half(c, step + 1, 0).start()
                    ring_half(c, step + 1, 1).start()

                low = (z + n_z - step) % n_z
                high = (z + step) % n_z
                weights = jnp.concatenate([wbuf[low], wbuf[high]], axis=1)
                blocks = jnp.concatenate([att[low, c], att[high, c]], axis=0)
                acc[c] += jnp.dot(weights, blocks, preferred_element_type=F32)

            @pl.when(step == half)
            def _():
                ring_half(c, step, 0).wait_recv()
                ring_half(c, step, 1).wait_recv()
                far = (z + half) % n_z
                acc[c] += jnp.dot(wbuf[far], att[far, c], preferred_element_type=F32)
                rs_send[c] = acc[c, rows : 2 * rows].astype(BF16)
                rs_copy(c).start()

            @pl.when(step == half + 1)
            def _():
                finish_block(c)

            @pl.when(step == half + 2)
            def _():
                share_out(c)

    whole(z_recv.at[pl.ds(0, n_z - 1)], z_rsem).wait()
    total = z_recv[0].astype(F32)
    for i in range(1, n_z):
        total = total + z_recv[i].astype(F32)
    velocity = (total * lax.rsqrt(sum_squares_lanes(total) / d_out + 1e-06))[:, 0:64]
    vel_ref[...] = velocity
    level = jnp.full(velocity.shape, lev_ref[0].astype(F32), F32)
    delta = sigma_of(level + 1.0) - sigma_of(level)
    n_send[:, 0:64] = lat_ref[...] + delta * velocity
    n_send[:, 64:128] = jnp.zeros_like(velocity)
    onward = pltpu.make_async_remote_copy(
        src_ref=n_send, dst_ref=n_recv, send_sem=n_ssem, recv_sem=n_rsem, device_id=(after, me), device_id_type=MESH
    )
    onward.start()

    whole(qkv.at[pl.ds(1, 2), pl.ds(0, others)], kv_send).wait()
    whole(qkv.at[pl.ds(0, 1), pl.ds(0, others)], q_send).wait()
    whole(wbuf.at[:, pl.ds(rows, rows)], w_send).wait()

    @pl.loop(0, n_chunks)
    def _(c):
        @pl.loop(1, half)
        def _(step):
            ring_full(c, step, 0).wait_send()
            ring_full(c, step, 1).wait_send()

        ring_half(c, half, 0).wait_send()
        ring_half(c, half, 1).wait_send()
        rs_copy(c).wait_send()
        y_copy(c).wait_send()
        for i in range(own_z):

            @pl.when(c * own_z + i != z)
            def _():
                z_copy(c, i).wait_send()

    onward.wait()
    next_ref[...] = jnp.where(group == 0, fresh_ref[...], n_recv[:, 0:64])


def solution(mesh):
    n_queue, n_seq = mesh.shape["queue"], mesh.shape["seq"]
    n_z = n_seq // 2
    n_chunks = 4 if n_z >= 8 else 2

    def on_device(projected, out_weight, head_weight, hidden_in, latent, fresh_noise, levels):
        tok, width = projected.shape[1:]
        hd = width // n_seq
        rows, n_tok = hidden_in.shape
        chunk = n_tok // n_chunks
        own_z = n_z // n_chunks
        half = n_z // 2
        vmem = pl.BlockSpec(memory_space=pltpu.VMEM)
        hbm = pl.BlockSpec(memory_space=pl.ANY)
        dma = pltpu.SemaphoreType.DMA
        return pl.pallas_call(
            functools.partial(kernel, n_queue, n_z, n_chunks, rows * n_seq),
            out_shape=(
                jax.ShapeDtypeStruct((rows, n_tok), F32),
                jax.ShapeDtypeStruct((tok, 64), F32),
                jax.ShapeDtypeStruct((tok, 64), F32),
            ),
            in_specs=[hbm, hbm, vmem, vmem, vmem, vmem, pl.BlockSpec(memory_space=pltpu.SMEM)],
            out_specs=(vmem, vmem, vmem),
            scratch_shapes=[
                pltpu.VMEM((3, tok, width), BF16),
                pltpu.VMEM((3, n_tok, hd), BF16),
                pltpu.VMEM((hd, n_tok), BF16),
                pltpu.VMEM((n_tok, chunk), F32),
                pltpu.VMEM((n_z, n_chunks, hd, chunk), BF16),
                pltpu.VMEM((n_z, 2 * rows, hd), BF16),
                pltpu.VMEM((n_chunks, 2 * rows, chunk), F32),
                pltpu.VMEM((rows, 128), BF16),
                pltpu.VMEM((n_chunks, rows, chunk), BF16),
                pltpu.VMEM((n_chunks, rows, chunk), BF16),
                pltpu.VMEM((n_chunks, 2, own_z, tok, 128), F32),
                pltpu.VMEM((n_chunks, own_z, tok, 128), F32),
                pltpu.VMEM((n_chunks, own_z, tok, 128), BF16),
                pltpu.VMEM((n_z, tok, 128), BF16),
                pltpu.VMEM((tok, 128), F32),
                pltpu.VMEM((tok, 128), F32),
                dma, dma, dma, dma, dma, dma, dma, dma, dma,
                dma((2, n_chunks, half + 1)),
                dma((2, n_chunks, half + 1)),
                dma((n_chunks,)),
                dma((n_chunks,)),
                dma((n_chunks,)),
                dma((n_chunks,)),
                dma((n_chunks, own_z)),
                dma,
                dma,
                dma,
            ],
            compiler_params=pltpu.CompilerParams(
                collective_id=0, has_side_effects=True, vmem_limit_bytes=48 * 1024 * 1024
            ),
        )(projected, out_weight, head_weight, hidden_in, latent, fresh_noise, levels)

    return jax.shard_map(
        on_device,
        mesh=mesh,
        in_specs=(
            P(None, ("queue", "seq"), None),
            P("seq", None),
            P("seq", None),
            P("seq", "queue"),
            P(("queue", "seq"), None),
            P("seq", None),
            P("queue"),
        ),
        out_specs=(P("seq", "queue"), P(("queue", "seq"), None), P(("queue", "seq"), None)),
        check_vma=False,
    )
```

```python
import functools
import math

import jax
import jax.numpy as jnp
from jax import lax
from jax.experimental import pallas as pl
from jax.experimental.pallas import tpu as pltpu
from jax.sharding import PartitionSpec as P

MESH = pl.DeviceIdType.MESH
F32 = jnp.float32
BF16 = jnp.bfloat16
STEPS = 50
SKEW = 1
LOG2E = 1.4426950408889634


def contract_last(a, b):
    return lax.dot_general(a, b, (((1,), (1,)), ((), ())), preferred_element_type=F32)


def sigma_of(level):
    frac = 1.0 - level / STEPS
    return 5.0 * frac / (1.0 + 4.0 * frac)


def kernel(
    n_queue, n_z, n_chunks, d_out,
    proj_hbm, w_hbm, hw_hbm, hid_hbm, lat_hbm, fresh_hbm, lev_ref,
    out_ref, vel_ref, next_ref,
    projv, qkv, vt, scores, att, wbuf, acc, hw_ref, hid_ref, lat_ref, fresh_ref, hwp, rs_send, rs_recv,
    sq_send, sq_recv, sq_column, pay, y_recv, z_send, z_recv, n_send, n_recv,
    proj_sem, small_sem, own_sem, kv_send, kv_recv, q_send, q_recv, w_own, w_send, w_recv, hw_send, hw_recv,
    ag_send, ag_recv, rs_ssem, rs_rsem, sq_ssem, sq_rsem, y_ssem, y_rsem, z_ssem, z_rsem, n_ssem, n_rsem,
):
    n_seq = 2 * n_z
    half = n_z // 2
    tok = projv.shape[1]
    hd = qkv.shape[2]
    n_tok = qkv.shape[1]
    chunk = n_tok // n_chunks
    lanes = math.gcd(chunk, 128)
    parts = chunk // lanes
    own_z = n_z // n_chunks
    rows = hid_ref.shape[0]
    group = lax.axis_index("queue")
    me = lax.axis_index("seq")
    z = me // 2
    y = me % 2
    partner = 2 * z + (1 - y)
    after = (group + 1) % n_queue
    before = (group + n_queue - 1) % n_queue

    barrier = pltpu.get_barrier_semaphore()
    load = pltpu.make_async_copy(proj_hbm, projv, proj_sem)
    load.start()

    @pl.loop(1, n_seq)
    def _(i):
        pl.semaphore_signal(barrier, inc=1, device_id=(group, (me + i) % n_seq), device_id_type=MESH)

    pl.semaphore_signal(barrier, inc=1, device_id=(after, me), device_id_type=MESH)
    pl.semaphore_signal(barrier, inc=1, device_id=(before, me), device_id_type=MESH)

    small = [
        pltpu.make_async_copy(src, dst, small_sem.at[i])
        for i, (src, dst) in enumerate(
            ((hw_hbm, hw_ref), (hid_hbm, hid_ref), (lat_hbm, lat_ref), (fresh_hbm, fresh_ref))
        )
    ]
    for copy in small:
        copy.start()

    @pl.loop(0, n_z)
    def _(i):
        pltpu.make_async_copy(
            w_hbm.at[:, pl.ds(pl.multiple_of((2 * i + y) * hd, hd), hd)], wbuf.at[i, pl.ds(0, rows)], w_own
        ).start()

    load.wait()
    small[0].wait()
    hwp[0:rows, 0:64] = hw_ref[...]
    hwp[0:rows, 64:128] = hw_ref[...]
    pl.semaphore_wait(barrier, n_seq + 1)

    def exchange(first, count, send_sem, recv_sem):
        def to(dest):
            pltpu.make_async_remote_copy(
                src_ref=projv.at[pl.ds(first, count), :, pl.ds(pl.multiple_of(dest * hd, hd), hd)],
                dst_ref=qkv.at[pl.ds(first, count), pl.ds(pl.multiple_of(me * tok, tok), tok), :],
                send_sem=send_sem,
                recv_sem=recv_sem,
                device_id=(group, dest),
                device_id_type=MESH,
            ).start()

        to(partner)

        @pl.loop(1, n_z)
        def _(i):
            far = n_z // 2 - i // 2
            shift = (1 - i % 2) * far + (i % 2) * (n_z - far)
            there = (z + shift) % n_z
            to(2 * there + y)
            to(2 * there + (1 - y))

    exchange(1, 2, kv_send, kv_recv)
    exchange(0, 1, q_send, q_recv)
    own = pltpu.make_async_copy(
        projv.at[:, :, pl.ds(pl.multiple_of(me * hd, hd), hd)],
        qkv.at[:, pl.ds(pl.multiple_of(me * tok, tok), tok), :],
        own_sem,
    )
    own.start()

    @pl.loop(0, n_z)
    def _(i):
        pltpu.make_async_remote_copy(
            src_ref=w_hbm.at[:, pl.ds(pl.multiple_of((2 * i + 1 - y) * hd, hd), hd)],
            dst_ref=wbuf.at[i, pl.ds(rows, rows)],
            send_sem=w_send,
            recv_sem=w_recv,
            device_id=(group, partner),
            device_id_type=MESH,
        ).start()

    hw_copy = pltpu.make_async_remote_copy(
        src_ref=hwp.at[pl.ds(0, rows)],
        dst_ref=hwp.at[pl.ds(rows, rows)],
        send_sem=hw_send,
        recv_sem=hw_recv,
        device_id=(group, partner),
        device_id_type=MESH,
    )
    hw_copy.start()

    def whole(ref, sem):
        return pltpu.make_async_copy(ref, ref, sem)

    others = (n_seq - 1) * tok
    for copy in small[1:]:
        copy.wait()
    own.wait()
    whole(qkv.at[pl.ds(1, 2), pl.ds(0, others)], kv_recv).wait()
    vt[...] = qkv[2].T
    whole(wbuf.at[:, pl.ds(0, rows)], w_own).wait()
    whole(wbuf.at[:, pl.ds(rows, rows)], w_recv).wait()
    hw_copy.wait_recv()
    whole(qkv.at[pl.ds(0, 1), pl.ds(0, others)], q_recv).wait()

    def ring(c, part, step, way):
        origin = (z + n_z - (step - 1)) % n_z if way == 0 else (z + step - 1) % n_z
        there = (z + 1) % n_z if way == 0 else (z + n_z - 1) % n_z

        def made(first, count):
            block = att.at[origin, c, pl.ds(first, count), pl.ds(part * lanes, lanes)]
            return pltpu.make_async_remote_copy(
                src_ref=block,
                dst_ref=block,
                send_sem=ag_send.at[way, c, part, step],
                recv_sem=ag_recv.at[way, c, part, step],
                device_id=(group, 2 * there + y),
                device_id_type=MESH,
            )

        return made

    def ring_full(c, part, step, way):
        return ring(c, part, step, way)(0, hd)

    def ring_half(c, part, step, way):
        return ring(c, part, step, way)(way * (hd // 2), hd // 2)

    key_block = math.gcd(256, n_tok)

    def attend(c):
        queries = qkv[0, pl.ds(pl.multiple_of(c * chunk, 16), chunk), :]
        peak = jnp.full((8, chunk), -jnp.inf, F32)
        for k in range(0, n_tok, key_block):
            part = contract_last(qkv[1, k : k + key_block, :], queries)
            scores[k : k + key_block, :] = part
            peak = jnp.maximum(peak, jnp.max(part.reshape(key_block // 8, 8, chunk), axis=0))
        peak = jnp.max(peak, axis=0, keepdims=True)
        total = jnp.zeros((8, chunk), F32)
        mixed = jnp.zeros((hd, chunk), F32)
        factor = LOG2E * hd ** (-0.5)
        for k in range(0, n_tok, key_block):
            raw = jnp.exp2((scores[k : k + key_block, :] - peak) * factor)
            total = total + jnp.sum(raw.reshape(key_block // 8, 8, chunk), axis=0)
            mixed = mixed + jnp.dot(vt[:, k : k + key_block], raw.astype(BF16), preferred_element_type=F32)
        total = jnp.sum(total, axis=0, keepdims=True)
        att[z, c] = (mixed / total).astype(BF16)

    def rs_copy(c, part):
        columns = pl.ds(part * lanes, lanes)
        return pltpu.make_async_remote_copy(
            src_ref=rs_send.at[c, :, columns],
            dst_ref=rs_recv.at[c, :, columns],
            send_sem=rs_ssem.at[c, part],
            recv_sem=rs_rsem.at[c, part],
            device_id=(group, partner),
            device_id_type=MESH,
        )

    def sq_copy(c, i):
        return pltpu.make_async_remote_copy(
            src_ref=sq_send.at[c],
            dst_ref=sq_recv.at[me],
            send_sem=sq_ssem.at[c, i],
            recv_sem=sq_rsem,
            device_id=(group, c * (2 * own_z) + i),
            device_id_type=MESH,
        )

    def y_copy(c):
        return pltpu.make_async_remote_copy(
            src_ref=pay.at[c, 1 - y],
            dst_ref=y_recv.at[c],
            send_sem=y_ssem.at[c],
            recv_sem=y_rsem.at[c],
            device_id=(group, partner),
            device_id_type=MESH,
        )

    def z_copy(c, i):
        return pltpu.make_async_remote_copy(
            src_ref=z_send.at[c, i],
            dst_ref=z_recv.at[z],
            send_sem=z_ssem.at[c, i],
            recv_sem=z_rsem,
            device_id=(group, 2 * (c * own_z + i) + y),
            device_id_type=MESH,
        )

    def part_velocity(c):
        turned = acc[c].T
        upper = turned.astype(BF16)
        lower = (turned - upper.astype(F32)).astype(BF16)
        vel = jnp.dot(upper, hwp[...], preferred_element_type=F32) + jnp.dot(lower, hwp[...], preferred_element_type=F32)
        vel = vel.reshape(own_z, 2, 2, tok // 2, 128)
        lane = lax.broadcasted_iota(jnp.int32, (tok // 2, 128), 1)
        for i in range(own_z):
            for k in range(2):
                pay[c, k, i] = jnp.where(lane < 64, vel[i, k, 0], vel[i, k, 1])
        y_copy(c).start()

    def finish_block(c):
        for part in range(parts):
            rs_copy(c, part).wait_recv()
            here = slice(part * lanes, (part + 1) * lanes)
            x = acc[c, 0:rows, here] + rs_recv[c, :, here].astype(F32)
            out_ref[:, pl.ds(pl.multiple_of(c * chunk + part * lanes, lanes), lanes)] = x
            sq_send[c, :, here] = jnp.sum(x * x, axis=0, keepdims=True)

        for i in range(2 * own_z):

            @pl.when(c * (2 * own_z) + i == me)
            def _():
                sq_recv[me] = sq_send[c]

            @pl.when(c * (2 * own_z) + i != me)
            def _():
                sq_copy(c, i).start()

    def share_out(c):
        y_copy(c).wait_recv()
        for i in range(own_z):
            total = pay[c, y, i] + y_recv[c, i]
            z_send[c, i] = total

            @pl.when(c * own_z + i == z)
            def _():
                z_recv[z] = total

            @pl.when(c * own_z + i != z)
            def _():
                z_copy(c, i).start()

    @pl.loop(0, SKEW * (n_chunks - 1) + half + 3)
    def _(slot):
        @pl.loop(0, n_chunks)
        def _(c):
            step = slot - SKEW * c

            @pl.when(step == 0)
            def _():
                attend(c)
                for part in range(parts):
                    ring_full(c, part, 1, 0).start()
                    ring_full(c, part, 1, 1).start()
                first = jnp.dot(wbuf[z], att[z, c], preferred_element_type=F32)
                columns = pl.ds(pl.multiple_of(c * chunk, chunk), chunk)
                acc[c, 0:rows] = first[0:rows] + hid_ref[:, columns].astype(F32)
                acc[c, rows : 2 * rows] = first[rows : 2 * rows]

            @pl.when(jnp.logical_and(step >= 1, step < half))
            def _():
                for part in range(parts):
                    for way in range(2):
                        ring_full(c, part, step, way).wait_recv()

                        @pl.when(step < half - 1)
                        def _():
                            ring_full(c, part, step + 1, way).start()

                        @pl.when(step == half - 1)
                        def _():
                            ring_half(c, part, step + 1, way).start()

                low = (z + n_z - step) % n_z
                high = (z + step) % n_z
                weights = jnp.concatenate([wbuf[low], wbuf[high]], axis=1)
                blocks = jnp.concatenate([att[low, c], att[high, c]], axis=0)
                acc[c] += jnp.dot(weights, blocks, preferred_element_type=F32)

            @pl.when(step == half)
            def _():
                far = (z + half) % n_z
                for part in range(parts):
                    ring_half(c, part, step, 0).wait_recv()
                    ring_half(c, part, step, 1).wait_recv()
                    here = slice(part * lanes, (part + 1) * lanes)
                    last = acc[c, :, here] + jnp.dot(wbuf[far], att[far, c, :, here], preferred_element_type=F32)
                    acc[c, :, here] = last
                    rs_send[c, :, here] = last[rows : 2 * rows].astype(BF16)
                    rs_copy(c, part).start()
                part_velocity(c)

            @pl.when(step == half + 1)
            def _():
                finish_block(c)

            @pl.when(step == half + 2)
            def _():
                share_out(c)

    whole(z_recv.at[pl.ds(0, n_z - 1)], z_rsem).wait()
    total = z_recv[0]
    for i in range(1, n_z):
        total = total + z_recv[i]
    whole(sq_recv.at[pl.ds(0, n_seq - 1)], sq_rsem).wait()
    squares = jnp.sum(sq_recv[...], axis=0)
    sq_column[...] = jnp.broadcast_to(lax.rsqrt(squares / d_out + 1e-06), (128, chunk)).T
    scale = sq_column[pl.ds(pl.multiple_of(me % (2 * own_z) * tok, 8), tok), 0:64]
    velocity = jnp.concatenate([total[:, 0:64], total[:, 64:128]], axis=0) * scale
    vel_ref[...] = velocity
    level = jnp.full(velocity.shape, lev_ref[0].astype(F32), F32)
    delta = sigma_of(level + 1.0) - sigma_of(level)
    n_send[:, 0:64] = lat_ref[...] + delta * velocity
    n_send[:, 64:128] = jnp.zeros_like(velocity)
    onward = pltpu.make_async_remote_copy(
        src_ref=n_send, dst_ref=n_recv, send_sem=n_ssem, recv_sem=n_rsem, device_id=(after, me), device_id_type=MESH
    )
    onward.start()

    whole(qkv.at[pl.ds(1, 2), pl.ds(0, others)], kv_send).wait()
    whole(qkv.at[pl.ds(0, 1), pl.ds(0, others)], q_send).wait()
    whole(wbuf.at[:, pl.ds(rows, rows)], w_send).wait()
    hw_copy.wait_send()

    @pl.loop(0, n_chunks)
    def _(c):
        for part in range(parts):

            @pl.loop(1, half)
            def _(step):
                ring_full(c, part, step, 0).wait_send()
                ring_full(c, part, step, 1).wait_send()

            ring_half(c, part, half, 0).wait_send()
            ring_half(c, part, half, 1).wait_send()
            rs_copy(c, part).wait_send()
        y_copy(c).wait_send()
        for i in range(own_z):

            @pl.when(c * own_z + i != z)
            def _():
                z_copy(c, i).wait_send()

        for i in range(2 * own_z):

            @pl.when(c * (2 * own_z) + i != me)
            def _():
                sq_copy(c, i).wait_send()

    onward.wait()
    next_ref[...] = jnp.where(group == 0, fresh_ref[...], n_recv[:, 0:64])


def solution(mesh):
    n_queue, n_seq = mesh.shape["queue"], mesh.shape["seq"]
    n_z = n_seq // 2
    n_chunks = 4 if n_z >= 8 else 2

    def on_device(projected, out_weight, head_weight, hidden_in, latent, fresh_noise, levels):
        tok, width = projected.shape[1:]
        hd = width // n_seq
        rows, n_tok = hidden_in.shape
        chunk = n_tok // n_chunks
        own_z = n_z // n_chunks
        half = n_z // 2
        parts = chunk // math.gcd(chunk, 128)
        vmem = pl.BlockSpec(memory_space=pltpu.VMEM)
        hbm = pl.BlockSpec(memory_space=pltpu.HBM)
        dma = pltpu.SemaphoreType.DMA
        return pl.pallas_call(
            functools.partial(kernel, n_queue, n_z, n_chunks, rows * n_seq),
            out_shape=(
                jax.ShapeDtypeStruct((rows, n_tok), F32),
                jax.ShapeDtypeStruct((tok, 64), F32),
                jax.ShapeDtypeStruct((tok, 64), F32),
            ),
            in_specs=[hbm, hbm, hbm, hbm, hbm, hbm, pl.BlockSpec(memory_space=pltpu.SMEM)],
            out_specs=(vmem, vmem, vmem),
            scratch_shapes=[
                pltpu.VMEM((3, tok, width), BF16),
                pltpu.VMEM((3, n_tok, hd), BF16),
                pltpu.VMEM((hd, n_tok), BF16),
                pltpu.VMEM((n_tok, chunk), F32),
                pltpu.VMEM((n_z, n_chunks, hd, chunk), BF16),
                pltpu.VMEM((n_z, 2 * rows, hd), BF16),
                pltpu.VMEM((n_chunks, 2 * rows, chunk), F32),
                pltpu.VMEM((rows, 64), BF16),
                pltpu.VMEM((rows, n_tok), BF16),
                pltpu.VMEM((tok, 64), F32),
                pltpu.VMEM((tok, 64), F32),
                pltpu.VMEM((2 * rows, 128), BF16),
                pltpu.VMEM((n_chunks, rows, chunk), BF16),
                pltpu.VMEM((n_chunks, rows, chunk), BF16),
                pltpu.VMEM((n_chunks, 1, chunk), F32),
                pltpu.VMEM((n_seq, 1, chunk), F32),
                pltpu.VMEM((chunk, 128), F32),
                pltpu.VMEM((n_chunks, 2, own_z, tok // 2, 128), F32),
                pltpu.VMEM((n_chunks, own_z, tok // 2, 128), F32),
                pltpu.VMEM((n_chunks, own_z, tok // 2, 128), F32),
                pltpu.VMEM((n_z, tok // 2, 128), F32),
                pltpu.VMEM((tok, 128), F32),
                pltpu.VMEM((tok, 128), F32),
                dma, dma((4,)), dma, dma, dma, dma, dma, dma, dma, dma, dma, dma,
                dma((2, n_chunks, parts, half + 1)),
                dma((2, n_chunks, parts, half + 1)),
                dma((n_chunks, parts)),
                dma((n_chunks, parts)),
                dma((n_chunks, 2 * own_z)),
                dma,
                dma((n_chunks,)),
                dma((n_chunks,)),
                dma((n_chunks, own_z)),
                dma,
                dma,
                dma,
            ],
            compiler_params=pltpu.CompilerParams(
                collective_id=0, has_side_effects=True, vmem_limit_bytes=48 * 1024 * 1024
            ),
        )(projected, out_weight, head_weight, hidden_in, latent, fresh_noise, levels)

    return jax.shard_map(
        on_device,
        mesh=mesh,
        in_specs=(
            P(None, ("queue", "seq"), None),
            P("seq", None),
            P("seq", None),
            P("seq", "queue"),
            P(("queue", "seq"), None),
            P("seq", None),
            P("queue"),
        ),
        out_specs=(P("seq", "queue"), P(("queue", "seq"), None), P(("queue", "seq"), None)),
        check_vma=False,
    )
```

```python
import functools
import math

import jax
import jax.numpy as jnp
from jax import lax
from jax.experimental import pallas as pl
from jax.experimental.pallas import tpu as pltpu
from jax.sharding import PartitionSpec as P

MESH = pl.DeviceIdType.MESH
F32 = jnp.float32
BF16 = jnp.bfloat16
STEPS = 50
PAIR = 2
LOG2E = 1.4426950408889634


def contract_last(a, b):
    return lax.dot_general(a, b, (((1,), (1,)), ((), ())), preferred_element_type=F32)


def sigma_of(level):
    frac = 1.0 - level / STEPS
    return 5.0 * frac / (1.0 + 4.0 * frac)


def kernel(
    n_queue, n_z, n_chunks, d_out,
    proj_hbm, w_hbm, hw_hbm, hid_hbm, lat_hbm, fresh_hbm, lev_ref,
    out_ref, vel_ref, next_ref,
    projv, qkv, vt, scores, att, wbuf, acc, hw_ref, hid_ref, lat_ref, fresh_ref, hwp, rs_send, rs_recv,
    sq_send, sq_recv, sq_column, pay, y_recv, z_send, z_recv, n_send, n_recv,
    proj_sem, small_sem, own_sem, kv_send, kv_recv, q_send, q_recv, w_own, w_send, w_recv, hw_send, hw_recv,
    ag_send, ag_recv, rs_ssem, rs_rsem, sq_ssem, sq_rsem, y_ssem, y_rsem, z_ssem, z_rsem, n_ssem, n_rsem,
):
    n_seq = 2 * n_z
    half = n_z // 2
    tok = projv.shape[1]
    hd = qkv.shape[2]
    n_tok = qkv.shape[1]
    chunk = n_tok // n_chunks
    lanes = math.gcd(chunk, 128)
    parts = chunk // lanes
    own_z = n_z // n_chunks
    rows = hid_ref.shape[0]
    group = lax.axis_index("queue")
    me = lax.axis_index("seq")
    z = me // 2
    y = me % 2
    partner = 2 * z + (1 - y)
    after = (group + 1) % n_queue
    before = (group + n_queue - 1) % n_queue

    barrier = pltpu.get_barrier_semaphore()
    load = pltpu.make_async_copy(proj_hbm, projv, proj_sem)
    load.start()

    @pl.loop(1, n_seq)
    def _(i):
        pl.semaphore_signal(barrier, inc=1, device_id=(group, (me + i) % n_seq), device_id_type=MESH)

    pl.semaphore_signal(barrier, inc=1, device_id=(after, me), device_id_type=MESH)
    pl.semaphore_signal(barrier, inc=1, device_id=(before, me), device_id_type=MESH)

    small = [
        pltpu.make_async_copy(src, dst, small_sem.at[i])
        for i, (src, dst) in enumerate(
            ((hw_hbm, hw_ref), (hid_hbm, hid_ref), (lat_hbm, lat_ref), (fresh_hbm, fresh_ref))
        )
    ]
    for copy in small:
        copy.start()

    @pl.loop(0, n_z)
    def _(i):
        pltpu.make_async_copy(
            w_hbm.at[:, pl.ds(pl.multiple_of((2 * i + y) * hd, hd), hd)], wbuf.at[i, pl.ds(0, rows)], w_own
        ).start()

    load.wait()
    small[0].wait()
    heads = hw_ref[...].astype(F32).T.astype(BF16)
    hwp[0:rows, 0:64] = heads
    hwp[0:rows, 64:128] = heads
    pl.semaphore_wait(barrier, n_seq + 1)

    def exchange(first, count, send_sem, recv_sem):
        def to(dest):
            pltpu.make_async_remote_copy(
                src_ref=projv.at[pl.ds(first, count), :, pl.ds(pl.multiple_of(dest * hd, hd), hd)],
                dst_ref=qkv.at[pl.ds(first, count), pl.ds(pl.multiple_of(me * tok, tok), tok), :],
                send_sem=send_sem,
                recv_sem=recv_sem,
                device_id=(group, dest),
                device_id_type=MESH,
            ).start()

        to(partner)

        @pl.loop(1, n_z)
        def _(i):
            far = n_z // 2 - i // 2
            shift = (1 - i % 2) * far + (i % 2) * (n_z - far)
            there = (z + shift) % n_z
            to(2 * there + y)
            to(2 * there + (1 - y))

    exchange(1, 2, kv_send, kv_recv)
    exchange(0, 1, q_send, q_recv)
    own = pltpu.make_async_copy(
        projv.at[:, :, pl.ds(pl.multiple_of(me * hd, hd), hd)],
        qkv.at[:, pl.ds(pl.multiple_of(me * tok, tok), tok), :],
        own_sem,
    )
    own.start()

    @pl.loop(0, n_z)
    def _(i):
        pltpu.make_async_remote_copy(
            src_ref=w_hbm.at[:, pl.ds(pl.multiple_of((2 * i + 1 - y) * hd, hd), hd)],
            dst_ref=wbuf.at[i, pl.ds(rows, rows)],
            send_sem=w_send,
            recv_sem=w_recv,
            device_id=(group, partner),
            device_id_type=MESH,
        ).start()

    hw_copy = pltpu.make_async_remote_copy(
        src_ref=hwp.at[pl.ds(0, rows)],
        dst_ref=hwp.at[pl.ds(rows, rows)],
        send_sem=hw_send,
        recv_sem=hw_recv,
        device_id=(group, partner),
        device_id_type=MESH,
    )
    hw_copy.start()

    def whole(ref, sem):
        return pltpu.make_async_copy(ref, ref, sem)

    others = (n_seq - 1) * tok
    for copy in small[1:]:
        copy.wait()
    own.wait()
    whole(qkv.at[pl.ds(1, 2), pl.ds(0, others)], kv_recv).wait()
    vt[...] = qkv[2].T
    whole(wbuf.at[:, pl.ds(0, rows)], w_own).wait()
    whole(wbuf.at[:, pl.ds(rows, rows)], w_recv).wait()
    hw_copy.wait_recv()
    whole(qkv.at[pl.ds(0, 1), pl.ds(0, others)], q_recv).wait()

    def ring(c, part, step, way):
        origin = (z + n_z - (step - 1)) % n_z if way == 0 else (z + step - 1) % n_z
        there = (z + 1) % n_z if way == 0 else (z + n_z - 1) % n_z

        def made(first, count):
            block = att.at[origin, c, pl.ds(first, count), pl.ds(part * lanes, lanes)]
            return pltpu.make_async_remote_copy(
                src_ref=block,
                dst_ref=block,
                send_sem=ag_send.at[way],
                recv_sem=ag_recv.at[way, c, part, step % 3],
                device_id=(group, 2 * there + y),
                device_id_type=MESH,
            )

        return made

    def ring_full(c, part, step, way):
        return ring(c, part, step, way)(0, hd)

    def ring_half(c, part, step, way):
        return ring(c, part, step, way)(way * (hd // 2), hd // 2)

    key_block = math.gcd(256, n_tok)

    def attend(c):
        queries = qkv[0, pl.ds(pl.multiple_of(c * chunk, 16), chunk), :]
        peak = jnp.full((8, chunk), -jnp.inf, F32)
        for k in range(0, n_tok, key_block):
            part = contract_last(qkv[1, k : k + key_block, :], queries)
            scores[k : k + key_block, :] = part
            peak = jnp.maximum(peak, jnp.max(part.reshape(key_block // 8, 8, chunk), axis=0))
        peak = jnp.max(peak, axis=0, keepdims=True)
        total = jnp.zeros((8, chunk), F32)
        mixed = jnp.zeros((hd, chunk), F32)
        factor = LOG2E * hd ** (-0.5)
        for k in range(0, n_tok, key_block):
            raw = jnp.exp2((scores[k : k + key_block, :] - peak) * factor)
            total = total + jnp.sum(raw.reshape(key_block // 8, 8, chunk), axis=0)
            mixed = mixed + jnp.dot(vt[:, k : k + key_block], raw.astype(BF16), preferred_element_type=F32)
        total = jnp.sum(total, axis=0, keepdims=True)
        att[z, c] = (mixed / total).astype(BF16)

    def rs_copy(c, part):
        columns = pl.ds(part * lanes, lanes)
        return pltpu.make_async_remote_copy(
            src_ref=rs_send.at[c, :, columns],
            dst_ref=rs_recv.at[c, :, columns],
            send_sem=rs_ssem,
            recv_sem=rs_rsem.at[c, part],
            device_id=(group, partner),
            device_id_type=MESH,
        )

    def sq_copy(c, i):
        return pltpu.make_async_remote_copy(
            src_ref=sq_send.at[c],
            dst_ref=sq_recv.at[me],
            send_sem=sq_ssem,
            recv_sem=sq_rsem,
            device_id=(group, c * (2 * own_z) + i),
            device_id_type=MESH,
        )

    def y_copy(c):
        return pltpu.make_async_remote_copy(
            src_ref=pay.at[c, 1 - y],
            dst_ref=y_recv.at[c],
            send_sem=y_ssem,
            recv_sem=y_rsem.at[c],
            device_id=(group, partner),
            device_id_type=MESH,
        )

    def z_copy(c, i):
        return pltpu.make_async_remote_copy(
            src_ref=z_send.at[c, i],
            dst_ref=z_recv.at[z],
            send_sem=z_ssem,
            recv_sem=z_rsem,
            device_id=(group, 2 * (c * own_z + i) + y),
            device_id_type=MESH,
        )

    def part_velocity(c):
        turned = acc[c].T
        upper = turned.astype(BF16)
        lower = (turned - upper.astype(F32)).astype(BF16)
        vel = jnp.dot(upper, hwp[...], preferred_element_type=F32) + jnp.dot(lower, hwp[...], preferred_element_type=F32)
        vel = vel.reshape(own_z, 2, 2, tok // 2, 128)
        lane = lax.broadcasted_iota(jnp.int32, (tok // 2, 128), 1)
        for i in range(own_z):
            for k in range(2):
                pay[c, k, i] = jnp.where(lane < 64, vel[i, k, 0], vel[i, k, 1])
        y_copy(c).start()

    def finish_block(c):
        for part in range(parts):
            rs_copy(c, part).wait_recv()
            here = slice(part * lanes, (part + 1) * lanes)
            x = acc[c, 0:rows, here] + rs_recv[c, :, here].astype(F32)
            out_ref[:, pl.ds(pl.multiple_of(c * chunk + part * lanes, lanes), lanes)] = x
            sq_send[c, :, here] = jnp.sum(x * x, axis=0, keepdims=True)

        for i in range(2 * own_z):

            @pl.when(c * (2 * own_z) + i == me)
            def _():
                sq_recv[me] = sq_send[c]

            @pl.when(c * (2 * own_z) + i != me)
            def _():
                sq_copy(c, i).start()

    def share_out(c):
        y_copy(c).wait_recv()
        for i in range(own_z):
            total = pay[c, y, i] + y_recv[c, i]
            padded = jnp.concatenate([total, jnp.zeros((8, 128), F32)], axis=0).astype(BF16)
            z_send[c, i] = padded

            @pl.when(c * own_z + i == z)
            def _():
                z_recv[z] = padded

            @pl.when(c * own_z + i != z)
            def _():
                z_copy(c, i).start()

    @pl.loop(0, (n_chunks - 1) // PAIR + half + 3)
    def _(slot):
        @pl.loop(0, n_chunks)
        def _(c):
            step = slot - c // PAIR

            @pl.when(step == 0)
            def _():
                attend(c)
                for part in range(parts):
                    ring_full(c, part, 1, 0).start()
                    ring_full(c, part, 1, 1).start()
                first = jnp.dot(wbuf[z], att[z, c], preferred_element_type=F32)
                columns = pl.ds(pl.multiple_of(c * chunk, chunk), chunk)
                acc[c, 0:rows] = first[0:rows] + hid_ref[:, columns].astype(F32)
                acc[c, rows : 2 * rows] = first[rows : 2 * rows]

            @pl.when(jnp.logical_and(step >= 1, step < half))
            def _():
                for part in range(parts):
                    for way in range(2):
                        ring_full(c, part, step, way).wait_recv()

                        @pl.when(step < half - 1)
                        def _():
                            ring_full(c, part, step + 1, way).start()

                        @pl.when(step == half - 1)
                        def _():
                            ring_half(c, part, step + 1, way).start()

                low = (z + n_z - step) % n_z
                high = (z + step) % n_z
                weights = jnp.concatenate([wbuf[low], wbuf[high]], axis=1)
                blocks = jnp.concatenate([att[low, c], att[high, c]], axis=0)
                acc[c] += jnp.dot(weights, blocks, preferred_element_type=F32)

            @pl.when(step == half)
            def _():
                far = (z + half) % n_z
                for part in range(parts):
                    ring_half(c, part, step, 0).wait_recv()
                    ring_half(c, part, step, 1).wait_recv()
                    here = slice(part * lanes, (part + 1) * lanes)
                    last = acc[c, :, here] + jnp.dot(wbuf[far], att[far, c, :, here], preferred_element_type=F32)
                    acc[c, :, here] = last
                    rs_send[c, :, here] = last[rows : 2 * rows].astype(BF16)
                    rs_copy(c, part).start()
                part_velocity(c)

            @pl.when(step == half + 1)
            def _():
                finish_block(c)

            @pl.when(step == half + 2)
            def _():
                share_out(c)

    whole(z_recv.at[pl.ds(0, n_z - 1)], z_rsem).wait()
    total = z_recv[0].astype(F32)
    for i in range(1, n_z):
        total = total + z_recv[i].astype(F32)
    total = total[0 : tok // 2]
    whole(sq_recv.at[pl.ds(0, n_seq - 1)], sq_rsem).wait()
    squares = jnp.sum(sq_recv[...], axis=0)
    sq_column[...] = jnp.broadcast_to(lax.rsqrt(squares / d_out + 1e-06), (128, chunk)).T
    scale = sq_column[pl.ds(pl.multiple_of(me % (2 * own_z) * tok, 8), tok), 0:64]
    velocity = jnp.concatenate([total[:, 0:64], total[:, 64:128]], axis=0) * scale
    vel_ref[...] = velocity
    level = jnp.full(velocity.shape, lev_ref[0].astype(F32), F32)
    delta = sigma_of(level + 1.0) - sigma_of(level)
    n_send[:, 0:64] = lat_ref[...] + delta * velocity
    n_send[:, 64:128] = jnp.zeros_like(velocity)
    onward = pltpu.make_async_remote_copy(
        src_ref=n_send, dst_ref=n_recv, send_sem=n_ssem, recv_sem=n_rsem, device_id=(after, me), device_id_type=MESH
    )
    onward.start()

    whole(qkv.at[pl.ds(1, 2), pl.ds(0, others)], kv_send).wait()
    whole(qkv.at[pl.ds(0, 1), pl.ds(0, others)], q_send).wait()
    whole(wbuf.at[:, pl.ds(rows, rows)], w_send).wait()
    hw_copy.wait_send()

    for way in range(2):
        whole(att.at[pl.ds(0, half - 1)], ag_send.at[way]).wait()
        whole(att.at[0, :, pl.ds(0, hd // 2)], ag_send.at[way]).wait()
    whole(rs_recv, rs_ssem).wait()
    whole(y_recv, y_ssem).wait()
    whole(z_recv.at[pl.ds(0, n_z - 1)], z_ssem).wait()
    whole(sq_recv.at[pl.ds(0, n_seq - 1)], sq_ssem).wait()

    onward.wait()
    next_ref[...] = jnp.where(group == 0, fresh_ref[...], n_recv[:, 0:64])


def write_out(*refs):
    sems = refs[6]
    copies = [pltpu.make_async_copy(refs[i], refs[3 + i], sems.at[i]) for i in range(3)]
    for copy in copies:
        copy.start()
    for copy in copies:
        copy.wait()


def solution(mesh):
    n_queue, n_seq = mesh.shape["queue"], mesh.shape["seq"]
    n_z = n_seq // 2
    n_chunks = 4 if n_z >= 8 else 2

    def on_device(projected, out_weight, head_weight, hidden_in, latent, fresh_noise, levels):
        tok, width = projected.shape[1:]
        hd = width // n_seq
        rows, n_tok = hidden_in.shape
        chunk = n_tok // n_chunks
        own_z = n_z // n_chunks
        half = n_z // 2
        parts = chunk // math.gcd(chunk, 128)
        vmem = pl.BlockSpec(memory_space=pltpu.VMEM)
        hbm = pl.BlockSpec(memory_space=pltpu.HBM)
        dma = pltpu.SemaphoreType.DMA
        results = pl.pallas_call(
            functools.partial(kernel, n_queue, n_z, n_chunks, rows * n_seq),
            out_shape=(
                pltpu.VMEM((rows, n_tok), F32),
                pltpu.VMEM((tok, 64), F32),
                pltpu.VMEM((tok, 64), F32),
            ),
            in_specs=[hbm, hbm, hbm, hbm, hbm, hbm, pl.BlockSpec(memory_space=pltpu.SMEM)],
            out_specs=(vmem, vmem, vmem),
            scratch_shapes=[
                pltpu.VMEM((3, tok, width), BF16),
                pltpu.VMEM((3, n_tok, hd), BF16),
                pltpu.VMEM((hd, n_tok), BF16),
                pltpu.VMEM((n_tok, chunk), F32),
                pltpu.VMEM((n_z, n_chunks, hd, chunk), BF16),
                pltpu.VMEM((n_z, 2 * rows, hd), BF16),
                pltpu.VMEM((n_chunks, 2 * rows, chunk), F32),
                pltpu.VMEM((64, rows), BF16),
                pltpu.VMEM((rows, n_tok), BF16),
                pltpu.VMEM((tok, 64), F32),
                pltpu.VMEM((tok, 64), F32),
                pltpu.VMEM((2 * rows, 128), BF16),
                pltpu.VMEM((n_chunks, rows, chunk), BF16),
                pltpu.VMEM((n_chunks, rows, chunk), BF16),
                pltpu.VMEM((n_chunks, 1, chunk), F32),
                pltpu.VMEM((n_seq, 1, chunk), F32),
                pltpu.VMEM((chunk, 128), F32),
                pltpu.VMEM((n_chunks, 2, own_z, tok // 2, 128), F32),
                pltpu.VMEM((n_chunks, own_z, tok // 2, 128), F32),
                pltpu.VMEM((n_chunks, own_z, tok // 2 + 8, 128), BF16),
                pltpu.VMEM((n_z, tok // 2 + 8, 128), BF16),
                pltpu.VMEM((tok, 128), F32),
                pltpu.VMEM((tok, 128), F32),
                dma, dma((4,)), dma, dma, dma, dma, dma, dma, dma, dma, dma, dma,
                dma((2,)),
                dma((2, n_chunks, parts, 3)),
                dma,
                dma((n_chunks, parts)),
                dma,
                dma,
                dma,
                dma((n_chunks,)),
                dma,
                dma,
                dma,
                dma,
            ],
            compiler_params=pltpu.CompilerParams(
                collective_id=0, has_side_effects=True, vmem_limit_bytes=62 * 1024 * 1024
            ),
        )(projected, out_weight, head_weight.T, hidden_in, latent, fresh_noise, levels)
        return pl.pallas_call(
            write_out,
            out_shape=tuple(jax.ShapeDtypeStruct(r.shape, r.dtype) for r in results),
            in_specs=[vmem] * 3,
            out_specs=(hbm, hbm, hbm),
            scratch_shapes=[dma((3,))],
        )(*results)

    return jax.shard_map(
        on_device,
        mesh=mesh,
        in_specs=(
            P(None, ("queue", "seq"), None),
            P("seq", None),
            P("seq", None),
            P("seq", "queue"),
            P(("queue", "seq"), None),
            P("seq", None),
            P("queue"),
        ),
        out_specs=(P("seq", "queue"), P(("queue", "seq"), None), P(("queue", "seq"), None)),
        check_vma=False,
    )
```

```python
import functools
import math

import jax
import jax.numpy as jnp
from jax import lax
from jax.experimental import pallas as pl
from jax.experimental.pallas import tpu as pltpu
from jax.sharding import PartitionSpec as P

MESH = pl.DeviceIdType.MESH
F32 = jnp.float32
BF16 = jnp.bfloat16
STEPS = 50
PAIR = 2
LOG2E = 1.4426950408889634


def contract_last(a, b):
    return lax.dot_general(a, b, (((1,), (1,)), ((), ())), preferred_element_type=F32)


def sigma_of(level):
    frac = 1.0 - level / STEPS
    return 5.0 * frac / (1.0 + 4.0 * frac)


def kernel(
    n_queue, n_z, n_chunks, d_out,
    proj_hbm, w_hbm, hw_hbm, hid_hbm, lat_hbm, fresh_hbm, lev_ref,
    out_ref, vel_ref, next_ref,
    projv, qkv, vt, scores, att, wbuf, acc, hw_ref, hid_ref, lat_ref, fresh_ref, hwp, rs_send, rs_recv,
    sq_send, sq_recv, sq_column, pay, y_recv, z_send, z_recv, n_send, n_recv,
    proj_sem, small_sem, own_sem, kv_send, kv_recv, q_send, q_recv, w_own, w_send, w_recv, hw_send, hw_recv,
    ag_send, ag_recv, rs_ssem, rs_rsem, sq_ssem, sq_rsem, y_ssem, y_rsem, z_ssem, z_rsem, n_ssem, n_rsem,
):
    n_seq = 2 * n_z
    half = n_z // 2
    tok = projv.shape[1]
    hd = qkv.shape[2]
    n_tok = qkv.shape[1]
    chunk = n_tok // n_chunks
    lanes = math.gcd(chunk, 128)
    parts = chunk // lanes
    own_z = n_z // n_chunks
    rows = hid_ref.shape[0]
    group = lax.axis_index("queue")
    me = lax.axis_index("seq")
    z = me // 2
    y = me % 2
    partner = 2 * z + (1 - y)
    after = (group + 1) % n_queue
    before = (group + n_queue - 1) % n_queue

    barrier = pltpu.get_barrier_semaphore()
    load = pltpu.make_async_copy(proj_hbm, projv, proj_sem)
    load.start()

    @pl.loop(1, n_seq)
    def _(i):
        pl.semaphore_signal(barrier, inc=1, device_id=(group, (me + i) % n_seq), device_id_type=MESH)

    pl.semaphore_signal(barrier, inc=1, device_id=(after, me), device_id_type=MESH)
    pl.semaphore_signal(barrier, inc=1, device_id=(before, me), device_id_type=MESH)

    small = [
        pltpu.make_async_copy(src, dst, small_sem.at[i])
        for i, (src, dst) in enumerate(
            ((hw_hbm, hw_ref), (hid_hbm, hid_ref), (lat_hbm, lat_ref), (fresh_hbm, fresh_ref))
        )
    ]
    for copy in small:
        copy.start()

    @pl.loop(0, n_z)
    def _(i):
        pltpu.make_async_copy(
            w_hbm.at[:, pl.ds(pl.multiple_of((2 * i + y) * hd, hd), hd)], wbuf.at[i, pl.ds(0, rows)], w_own
        ).start()

    load.wait()
    small[0].wait()
    heads = hw_ref[...].astype(F32).T.astype(BF16)
    hwp[0:rows, 0:64] = heads
    hwp[0:rows, 64:128] = heads
    pl.semaphore_wait(barrier, n_seq + 1)

    def exchange(first, count, send_sem, recv_sem):
        def to(dest):
            pltpu.make_async_remote_copy(
                src_ref=projv.at[pl.ds(first, count), :, pl.ds(pl.multiple_of(dest * hd, hd), hd)],
                dst_ref=qkv.at[pl.ds(first, count), pl.ds(pl.multiple_of(me * tok, tok), tok), :],
                send_sem=send_sem,
                recv_sem=recv_sem,
                device_id=(group, dest),
                device_id_type=MESH,
            ).start()

        to(partner)

        @pl.loop(1, n_z)
        def _(i):
            far = n_z // 2 - i // 2
            shift = (1 - i % 2) * far + (i % 2) * (n_z - far)
            there = (z + shift) % n_z
            to(2 * there + y)
            to(2 * there + (1 - y))

    exchange(1, 2, kv_send, kv_recv)
    exchange(0, 1, q_send, q_recv)
    own = pltpu.make_async_copy(
        projv.at[:, :, pl.ds(pl.multiple_of(me * hd, hd), hd)],
        qkv.at[:, pl.ds(pl.multiple_of(me * tok, tok), tok), :],
        own_sem,
    )
    own.start()

    @pl.loop(0, n_z)
    def _(i):
        pltpu.make_async_remote_copy(
            src_ref=w_hbm.at[:, pl.ds(pl.multiple_of((2 * i + 1 - y) * hd, hd), hd)],
            dst_ref=wbuf.at[i, pl.ds(rows, rows)],
            send_sem=w_send,
            recv_sem=w_recv,
            device_id=(group, partner),
            device_id_type=MESH,
        ).start()

    hw_copy = pltpu.make_async_remote_copy(
        src_ref=hwp.at[pl.ds(0, rows)],
        dst_ref=hwp.at[pl.ds(rows, rows)],
        send_sem=hw_send,
        recv_sem=hw_recv,
        device_id=(group, partner),
        device_id_type=MESH,
    )
    hw_copy.start()

    def whole(ref, sem):
        return pltpu.make_async_copy(ref, ref, sem)

    others = (n_seq - 1) * tok
    for copy in small[1:]:
        copy.wait()
    own.wait()
    whole(qkv.at[pl.ds(1, 2), pl.ds(0, others)], kv_recv).wait()
    vt[...] = qkv[2].T
    whole(wbuf.at[:, pl.ds(0, rows)], w_own).wait()
    whole(wbuf.at[:, pl.ds(rows, rows)], w_recv).wait()
    hw_copy.wait_recv()
    whole(qkv.at[pl.ds(0, 1), pl.ds(0, others)], q_recv).wait()

    def ring(c, part, step, way):
        origin = (z + n_z - (step - 1)) % n_z if way == 0 else (z + step - 1) % n_z
        there = (z + 1) % n_z if way == 0 else (z + n_z - 1) % n_z

        def made(first, count):
            block = att.at[origin, c, pl.ds(first, count), pl.ds(part * lanes, lanes)]
            return pltpu.make_async_remote_copy(
                src_ref=block,
                dst_ref=block,
                send_sem=ag_send.at[way],
                recv_sem=ag_recv.at[way, c, part, step % 3],
                device_id=(group, 2 * there + y),
                device_id_type=MESH,
            )

        return made

    def ring_full(c, part, step, way):
        return ring(c, part, step, way)(0, hd)

    def ring_half(c, part, step, way):
        return ring(c, part, step, way)(way * (hd // 2), hd // 2)

    key_block = math.gcd(256, n_tok)

    def attend(c):
        queries = qkv[0, pl.ds(pl.multiple_of(c * chunk, 16), chunk), :]
        peak = jnp.full((8, chunk), -jnp.inf, F32)
        for k in range(0, n_tok, key_block):
            part = contract_last(qkv[1, k : k + key_block, :], queries)
            scores[k : k + key_block, :] = part
            peak = jnp.maximum(peak, jnp.max(part.reshape(key_block // 8, 8, chunk), axis=0))
        peak = jnp.max(peak, axis=0, keepdims=True)
        total = jnp.zeros((8, chunk), F32)
        mixed = jnp.zeros((hd, chunk), F32)
        factor = LOG2E * hd ** (-0.5)
        for k in range(0, n_tok, key_block):
            raw = jnp.exp2((scores[k : k + key_block, :] - peak) * factor)
            total = total + jnp.sum(raw.reshape(key_block // 8, 8, chunk), axis=0)
            mixed = mixed + jnp.dot(vt[:, k : k + key_block], raw.astype(BF16), preferred_element_type=F32)
        total = jnp.sum(total, axis=0, keepdims=True)
        att[z, c] = (mixed / total).astype(BF16)

    def rs_copy(c, part):
        columns = pl.ds(part * lanes, lanes)
        return pltpu.make_async_remote_copy(
            src_ref=rs_send.at[c, :, columns],
            dst_ref=rs_recv.at[c, :, columns],
            send_sem=rs_ssem,
            recv_sem=rs_rsem.at[c, part],
            device_id=(group, partner),
            device_id_type=MESH,
        )

    def lanes_of(i):
        first = i * tok // lanes * lanes
        return pl.ds(first, -(-(i + 1) * tok // lanes) * lanes - first)

    def sq_copy(c, i):
        return pltpu.make_async_remote_copy(
            src_ref=sq_send.at[c, :, lanes_of(i)],
            dst_ref=sq_recv.at[me, :, lanes_of(i)],
            send_sem=sq_ssem,
            recv_sem=sq_rsem,
            device_id=(group, c * (2 * own_z) + i),
            device_id_type=MESH,
        )

    def y_copy(c):
        return pltpu.make_async_remote_copy(
            src_ref=pay.at[c, 1 - y],
            dst_ref=y_recv.at[c],
            send_sem=y_ssem,
            recv_sem=y_rsem.at[c],
            device_id=(group, partner),
            device_id_type=MESH,
        )

    def z_copy(c, i):
        return pltpu.make_async_remote_copy(
            src_ref=z_send.at[c, i],
            dst_ref=z_recv.at[z],
            send_sem=z_ssem,
            recv_sem=z_rsem,
            device_id=(group, 2 * (c * own_z + i) + y),
            device_id_type=MESH,
        )

    def part_velocity(c):
        turned = acc[c].T
        upper = turned.astype(BF16)
        lower = (turned - upper.astype(F32)).astype(BF16)
        vel = jnp.dot(upper, hwp[...], preferred_element_type=F32) + jnp.dot(lower, hwp[...], preferred_element_type=F32)
        vel = vel.reshape(own_z, 2, 2, tok // 2, 128)
        lane = lax.broadcasted_iota(jnp.int32, (tok // 2, 128), 1)
        for i in range(own_z):
            for k in range(2):
                pay[c, k, i] = jnp.where(lane < 64, vel[i, k, 0], vel[i, k, 1])
        y_copy(c).start()

    def finish_block(c):
        for part in range(parts):
            rs_copy(c, part).wait_recv()
            here = slice(part * lanes, (part + 1) * lanes)
            x = acc[c, 0:rows, here] + rs_recv[c, :, here].astype(F32)
            out_ref[:, pl.ds(pl.multiple_of(c * chunk + part * lanes, lanes), lanes)] = x
            sq_send[c, :, here] = jnp.sum(x * x, axis=0, keepdims=True)

        for i in range(2 * own_z):

            @pl.when(c * (2 * own_z) + i == me)
            def _():
                sq_recv[me] = sq_send[c]

            @pl.when(c * (2 * own_z) + i != me)
            def _():
                sq_copy(c, i).start()

    def share_out(c):
        y_copy(c).wait_recv()
        for i in range(own_z):
            total = pay[c, y, i] + y_recv[c, i]
            padded = jnp.concatenate([total, jnp.zeros((8, 128), F32)], axis=0).astype(BF16)
            z_send[c, i] = padded

            @pl.when(c * own_z + i == z)
            def _():
                z_recv[z] = padded

            @pl.when(c * own_z + i != z)
            def _():
                z_copy(c, i).start()

    @pl.loop(0, (n_chunks - 1) // PAIR + half + 3)
    def _(slot):
        @pl.loop(0, n_chunks)
        def _(c):
            step = slot - c // PAIR

            @pl.when(step == 0)
            def _():
                attend(c)
                for part in range(parts):
                    ring_full(c, part, 1, 0).start()
                    ring_full(c, part, 1, 1).start()
                first = jnp.dot(wbuf[z], att[z, c], preferred_element_type=F32)
                columns = pl.ds(pl.multiple_of(c * chunk, chunk), chunk)
                acc[c, 0:rows] = first[0:rows] + hid_ref[:, columns].astype(F32)
                acc[c, rows : 2 * rows] = first[rows : 2 * rows]

            @pl.when(jnp.logical_and(step >= 1, step < half))
            def _():
                for part in range(parts):
                    for way in range(2):
                        ring_full(c, part, step, way).wait_recv()

                        @pl.when(step < half - 1)
                        def _():
                            ring_full(c, part, step + 1, way).start()

                        @pl.when(step == half - 1)
                        def _():
                            ring_half(c, part, step + 1, way).start()

                low = (z + n_z - step) % n_z
                high = (z + step) % n_z
                weights = jnp.concatenate([wbuf[low], wbuf[high]], axis=1)
                blocks = jnp.concatenate([att[low, c], att[high, c]], axis=0)
                acc[c] += jnp.dot(weights, blocks, preferred_element_type=F32)

            @pl.when(step == half)
            def _():
                far = (z + half) % n_z
                for part in range(parts):
                    ring_half(c, part, step, 0).wait_recv()
                    ring_half(c, part, step, 1).wait_recv()
                    here = slice(part * lanes, (part + 1) * lanes)
                    last = acc[c, :, here] + jnp.dot(wbuf[far], att[far, c, :, here], preferred_element_type=F32)
                    acc[c, :, here] = last
                    rs_send[c, :, here] = last[rows : 2 * rows].astype(BF16)
                    rs_copy(c, part).start()
                part_velocity(c)

            @pl.when(step == half + 1)
            def _():
                finish_block(c)

            @pl.when(step == half + 2)
            def _():
                share_out(c)

    whole(z_recv.at[pl.ds(0, n_z - 1)], z_rsem).wait()
    total = z_recv[0].astype(F32)
    for i in range(1, n_z):
        total = total + z_recv[i].astype(F32)
    total = total[0 : tok // 2]
    for i in range(2 * own_z):

        @pl.when(me % (2 * own_z) == i)
        def _():
            whole(sq_recv.at[pl.ds(0, n_seq - 1), :, lanes_of(i)], sq_rsem).wait()

    squares = jnp.sum(sq_recv[...], axis=0)
    sq_column[...] = jnp.broadcast_to(lax.rsqrt(squares / d_out + 1e-06), (128, chunk)).T
    scale = sq_column[pl.ds(pl.multiple_of(me % (2 * own_z) * tok, 8), tok), 0:64]
    velocity = jnp.concatenate([total[:, 0:64], total[:, 64:128]], axis=0) * scale
    vel_ref[...] = velocity
    level = jnp.full(velocity.shape, lev_ref[0].astype(F32), F32)
    delta = sigma_of(level + 1.0) - sigma_of(level)
    n_send[:, 0:64] = lat_ref[...] + delta * velocity
    n_send[:, 64:128] = jnp.zeros_like(velocity)
    onward = pltpu.make_async_remote_copy(
        src_ref=n_send, dst_ref=n_recv, send_sem=n_ssem, recv_sem=n_rsem, device_id=(after, me), device_id_type=MESH
    )
    onward.start()

    whole(qkv.at[pl.ds(1, 2), pl.ds(0, others)], kv_send).wait()
    whole(qkv.at[pl.ds(0, 1), pl.ds(0, others)], q_send).wait()
    whole(wbuf.at[:, pl.ds(rows, rows)], w_send).wait()
    hw_copy.wait_send()

    for way in range(2):
        whole(att.at[pl.ds(0, half - 1)], ag_send.at[way]).wait()
        whole(att.at[0, :, pl.ds(0, hd // 2)], ag_send.at[way]).wait()
    whole(rs_recv, rs_ssem).wait()
    whole(y_recv, y_ssem).wait()
    whole(z_recv.at[pl.ds(0, n_z - 1)], z_ssem).wait()
    for i in range(2 * own_z):

        @pl.when(me % (2 * own_z) != i)
        def _():
            whole(sq_recv.at[pl.ds(0, n_chunks), :, lanes_of(i)], sq_ssem).wait()

        @pl.when(me % (2 * own_z) == i)
        def _():
            whole(sq_recv.at[pl.ds(0, n_chunks - 1), :, lanes_of(i)], sq_ssem).wait()


    onward.wait()
    next_ref[...] = jnp.where(group == 0, fresh_ref[...], n_recv[:, 0:64])


def write_out(*refs):
    sems = refs[6]
    copies = [pltpu.make_async_copy(refs[i], refs[3 + i], sems.at[i]) for i in range(3)]
    for copy in copies:
        copy.start()
    for copy in copies:
        copy.wait()


def solution(mesh):
    n_queue, n_seq = mesh.shape["queue"], mesh.shape["seq"]
    n_z = n_seq // 2
    n_chunks = 4 if n_z >= 8 else 2

    def on_device(projected, out_weight, head_weight, hidden_in, latent, fresh_noise, levels):
        tok, width = projected.shape[1:]
        hd = width // n_seq
        rows, n_tok = hidden_in.shape
        chunk = n_tok // n_chunks
        own_z = n_z // n_chunks
        half = n_z // 2
        parts = chunk // math.gcd(chunk, 128)
        vmem = pl.BlockSpec(memory_space=pltpu.VMEM)
        hbm = pl.BlockSpec(memory_space=pltpu.HBM)
        dma = pltpu.SemaphoreType.DMA
        results = pl.pallas_call(
            functools.partial(kernel, n_queue, n_z, n_chunks, rows * n_seq),
            out_shape=(
                pltpu.VMEM((rows, n_tok), F32),
                pltpu.VMEM((tok, 64), F32),
                pltpu.VMEM((tok, 64), F32),
            ),
            in_specs=[hbm, hbm, hbm, hbm, hbm, hbm, pl.BlockSpec(memory_space=pltpu.SMEM)],
            out_specs=(vmem, vmem, vmem),
            scratch_shapes=[
                pltpu.VMEM((3, tok, width), BF16),
                pltpu.VMEM((3, n_tok, hd), BF16),
                pltpu.VMEM((hd, n_tok), BF16),
                pltpu.VMEM((n_tok, chunk), F32),
                pltpu.VMEM((n_z, n_chunks, hd, chunk), BF16),
                pltpu.VMEM((n_z, 2 * rows, hd), BF16),
                pltpu.VMEM((n_chunks, 2 * rows, chunk), F32),
                pltpu.VMEM((64, rows), BF16),
                pltpu.VMEM((rows, n_tok), BF16),
                pltpu.VMEM((tok, 64), F32),
                pltpu.VMEM((tok, 64), F32),
                pltpu.VMEM((2 * rows, 128), BF16),
                pltpu.VMEM((n_chunks, rows, chunk), BF16),
                pltpu.VMEM((n_chunks, rows, chunk), BF16),
                pltpu.VMEM((n_chunks, 1, chunk), F32),
                pltpu.VMEM((n_seq, 1, chunk), F32),
                pltpu.VMEM((chunk, 128), F32),
                pltpu.VMEM((n_chunks, 2, own_z, tok // 2, 128), F32),
                pltpu.VMEM((n_chunks, own_z, tok // 2, 128), F32),
                pltpu.VMEM((n_chunks, own_z, tok // 2 + 8, 128), BF16),
                pltpu.VMEM((n_z, tok // 2 + 8, 128), BF16),
                pltpu.VMEM((tok, 128), F32),
                pltpu.VMEM((tok, 128), F32),
                dma, dma((4,)), dma, dma, dma, dma, dma, dma, dma, dma, dma, dma,
                dma((2,)),
                dma((2, n_chunks, parts, 3)),
                dma,
                dma((n_chunks, parts)),
                dma,
                dma,
                dma,
                dma((n_chunks,)),
                dma,
                dma,
                dma,
                dma,
            ],
            compiler_params=pltpu.CompilerParams(
                collective_id=0, has_side_effects=True, vmem_limit_bytes=62 * 1024 * 1024
            ),
        )(projected, out_weight, head_weight.T, hidden_in, latent, fresh_noise, levels)
        return pl.pallas_call(
            write_out,
            out_shape=tuple(jax.ShapeDtypeStruct(r.shape, r.dtype) for r in results),
            in_specs=[vmem] * 3,
            out_specs=(hbm, hbm, hbm),
            scratch_shapes=[dma((3,))],
            compiler_params=pltpu.CompilerParams(vmem_limit_bytes=4 * 1024 * 1024),
        )(*results)

    return jax.shard_map(
        on_device,
        mesh=mesh,
        in_specs=(
            P(None, ("queue", "seq"), None),
            P("seq", None),
            P("seq", None),
            P("seq", "queue"),
            P(("queue", "seq"), None),
            P("seq", None),
            P("queue"),
        ),
        out_specs=(P("seq", "queue"), P(("queue", "seq"), None), P(("queue", "seq"), None)),
        check_vma=False,
    )
```

```python
import functools
import math

import jax
import jax.numpy as jnp
from jax import lax
from jax.experimental import pallas as pl
from jax.experimental.pallas import tpu as pltpu
from jax.sharding import PartitionSpec as P

MESH = pl.DeviceIdType.MESH
F32 = jnp.float32
BF16 = jnp.bfloat16
STEPS = 50
PAIR = 2
LOG2E = 1.4426950408889634


def contract_last(a, b):
    return lax.dot_general(a, b, (((1,), (1,)), ((), ())), preferred_element_type=F32)


def sigma_of(level):
    frac = 1.0 - level / STEPS
    return 5.0 * frac / (1.0 + 4.0 * frac)


def kernel(
    n_queue, n_z, n_chunks, d_out,
    proj_hbm, w_hbm, hw_hbm, hid_hbm, lat_hbm, fresh_hbm, lev_ref,
    out_ref, vel_ref, next_ref,
    projv, qkv, vt, scores, att, wbuf, acc, hw_ref, hid_ref, lat_ref, fresh_ref, hwp, rs_send, rs_recv,
    sq_send, sq_recv, sq_column, pay, y_recv, z_send, z_recv, n_send, n_recv,
    proj_sem, small_sem, own_sem, kv_send, kv_recv, q_send, q_recv, w_own, w_send, w_recv, hw_send, hw_recv,
    ag_send, ag_recv, rs_ssem, rs_rsem, sq_ssem, sq_rsem, y_ssem, y_rsem, z_ssem, z_rsem, n_ssem, n_rsem,
):
    n_seq = 2 * n_z
    half = n_z // 2
    tok = projv.shape[1]
    hd = qkv.shape[2]
    n_tok = qkv.shape[1]
    chunk = n_tok // n_chunks
    lanes = math.gcd(chunk, 128)
    parts = chunk // lanes
    own_z = n_z // n_chunks
    rows = hid_ref.shape[0]
    group = lax.axis_index("queue")
    me = lax.axis_index("seq")
    z = me // 2
    y = me % 2
    partner = 2 * z + (1 - y)
    after = (group + 1) % n_queue
    before = (group + n_queue - 1) % n_queue

    barrier = pltpu.get_barrier_semaphore()
    load = pltpu.make_async_copy(proj_hbm, projv, proj_sem)
    load.start()

    @pl.loop(1, n_seq)
    def _(i):
        pl.semaphore_signal(barrier, inc=1, device_id=(group, (me + i) % n_seq), device_id_type=MESH)

    pl.semaphore_signal(barrier, inc=1, device_id=(after, me), device_id_type=MESH)
    pl.semaphore_signal(barrier, inc=1, device_id=(before, me), device_id_type=MESH)

    small = [
        pltpu.make_async_copy(src, dst, small_sem.at[i])
        for i, (src, dst) in enumerate(
            ((hw_hbm, hw_ref), (hid_hbm, hid_ref), (lat_hbm, lat_ref), (fresh_hbm, fresh_ref))
        )
    ]
    for copy in small:
        copy.start()

    @pl.loop(0, n_z)
    def _(i):
        pltpu.make_async_copy(
            w_hbm.at[:, pl.ds(pl.multiple_of((2 * i + y) * hd, hd), hd)], wbuf.at[i, pl.ds(0, rows)], w_own
        ).start()

    load.wait()
    small[0].wait()
    heads = hw_ref[...].astype(F32).T.astype(BF16)
    hwp[0:rows, 0:64] = heads
    hwp[0:rows, 64:128] = heads
    pl.semaphore_wait(barrier, n_seq + 1)

    def exchange(first, count, send_sem, recv_sem):
        def to(dest):
            pltpu.make_async_remote_copy(
                src_ref=projv.at[pl.ds(first, count), :, pl.ds(pl.multiple_of(dest * hd, hd), hd)],
                dst_ref=qkv.at[pl.ds(first, count), pl.ds(pl.multiple_of(me * tok, tok), tok), :],
                send_sem=send_sem,
                recv_sem=recv_sem,
                device_id=(group, dest),
                device_id_type=MESH,
            ).start()

        to(partner)

        @pl.loop(1, n_z)
        def _(i):
            far = n_z // 2 - i // 2
            shift = (1 - i % 2) * far + (i % 2) * (n_z - far)
            there = (z + shift) % n_z
            to(2 * there + y)
            to(2 * there + (1 - y))

    exchange(1, 2, kv_send, kv_recv)
    exchange(0, 1, q_send, q_recv)
    own = pltpu.make_async_copy(
        projv.at[:, :, pl.ds(pl.multiple_of(me * hd, hd), hd)],
        qkv.at[:, pl.ds(pl.multiple_of(me * tok, tok), tok), :],
        own_sem,
    )
    own.start()

    @pl.loop(0, n_z)
    def _(i):
        pltpu.make_async_remote_copy(
            src_ref=w_hbm.at[:, pl.ds(pl.multiple_of((2 * i + 1 - y) * hd, hd), hd)],
            dst_ref=wbuf.at[i, pl.ds(rows, rows)],
            send_sem=w_send,
            recv_sem=w_recv,
            device_id=(group, partner),
            device_id_type=MESH,
        ).start()

    hw_copy = pltpu.make_async_remote_copy(
        src_ref=hwp.at[pl.ds(0, rows)],
        dst_ref=hwp.at[pl.ds(rows, rows)],
        send_sem=hw_send,
        recv_sem=hw_recv,
        device_id=(group, partner),
        device_id_type=MESH,
    )
    hw_copy.start()

    def whole(ref, sem):
        return pltpu.make_async_copy(ref, ref, sem)

    others = (n_seq - 1) * tok
    for copy in small[1:]:
        copy.wait()
    own.wait()
    whole(qkv.at[pl.ds(1, 2), pl.ds(0, others)], kv_recv).wait()
    vt[...] = qkv[2].T
    whole(wbuf.at[:, pl.ds(0, rows)], w_own).wait()
    whole(wbuf.at[:, pl.ds(rows, rows)], w_recv).wait()
    hw_copy.wait_recv()
    whole(qkv.at[pl.ds(0, 1), pl.ds(0, others)], q_recv).wait()

    def ring(c, part, step, way):
        origin = (z + n_z - (step - 1)) % n_z if way == 0 else (z + step - 1) % n_z
        there = (z + 1) % n_z if way == 0 else (z + n_z - 1) % n_z

        def made(first, count):
            block = att.at[origin, c, pl.ds(first, count), pl.ds(part * lanes, lanes)]
            return pltpu.make_async_remote_copy(
                src_ref=block,
                dst_ref=block,
                send_sem=ag_send.at[way],
                recv_sem=ag_recv.at[way, c, part, step % 3],
                device_id=(group, 2 * there + y),
                device_id_type=MESH,
            )

        return made

    def ring_full(c, part, step, way):
        return ring(c, part, step, way)(0, hd)

    def ring_half(c, part, step, way):
        return ring(c, part, step, way)(way * (hd // 2), hd // 2)

    key_block = math.gcd(256, n_tok)

    def attend(c, part):
        queries = qkv[0, pl.ds(pl.multiple_of(c * chunk + part * lanes, 16), lanes), :]
        peak = jnp.full((8, lanes), -jnp.inf, F32)
        for k in range(0, n_tok, key_block):
            some = contract_last(qkv[1, k : k + key_block, :], queries)
            scores[k : k + key_block, :] = some
            peak = jnp.maximum(peak, jnp.max(some.reshape(key_block // 8, 8, lanes), axis=0))
        peak = jnp.max(peak, axis=0, keepdims=True)
        total = jnp.zeros((8, lanes), F32)
        mixed = jnp.zeros((hd, lanes), F32)
        factor = LOG2E * hd ** (-0.5)
        for k in range(0, n_tok, key_block):
            raw = jnp.exp2((scores[k : k + key_block, :] - peak) * factor)
            total = total + jnp.sum(raw.reshape(key_block // 8, 8, lanes), axis=0)
            mixed = mixed + jnp.dot(vt[:, k : k + key_block], raw.astype(BF16), preferred_element_type=F32)
        total = jnp.sum(total, axis=0, keepdims=True)
        att[z, c, :, part * lanes : (part + 1) * lanes] = (mixed / total).astype(BF16)

    def rs_copy(c, part):
        columns = pl.ds(part * lanes, lanes)
        return pltpu.make_async_remote_copy(
            src_ref=rs_send.at[c, :, columns],
            dst_ref=rs_recv.at[c, :, columns],
            send_sem=rs_ssem,
            recv_sem=rs_rsem.at[c, part],
            device_id=(group, partner),
            device_id_type=MESH,
        )

    def lanes_of(i):
        first = i * tok // lanes * lanes
        return pl.ds(first, -(-(i + 1) * tok // lanes) * lanes - first)

    def sq_copy(c, i):
        return pltpu.make_async_remote_copy(
            src_ref=sq_send.at[c, :, lanes_of(i)],
            dst_ref=sq_recv.at[me, :, lanes_of(i)],
            send_sem=sq_ssem,
            recv_sem=sq_rsem,
            device_id=(group, c * (2 * own_z) + i),
            device_id_type=MESH,
        )

    def y_copy(c):
        return pltpu.make_async_remote_copy(
            src_ref=pay.at[c, 1 - y],
            dst_ref=y_recv.at[c],
            send_sem=y_ssem,
            recv_sem=y_rsem.at[c],
            device_id=(group, partner),
            device_id_type=MESH,
        )

    def z_copy(c, i):
        return pltpu.make_async_remote_copy(
            src_ref=z_send.at[c, i],
            dst_ref=z_recv.at[z],
            send_sem=z_ssem,
            recv_sem=z_rsem,
            device_id=(group, 2 * (c * own_z + i) + y),
            device_id_type=MESH,
        )

    def part_velocity(c):
        turned = acc[c].T
        upper = turned.astype(BF16)
        lower = (turned - upper.astype(F32)).astype(BF16)
        vel = jnp.dot(upper, hwp[...], preferred_element_type=F32) + jnp.dot(lower, hwp[...], preferred_element_type=F32)
        vel = vel.reshape(own_z, 2, 2, tok // 2, 128)
        lane = lax.broadcasted_iota(jnp.int32, (tok // 2, 128), 1)
        for i in range(own_z):
            for k in range(2):
                pay[c, k, i] = jnp.where(lane < 64, vel[i, k, 0], vel[i, k, 1])
        y_copy(c).start()

    def finish_block(c):
        for part in range(parts):
            rs_copy(c, part).wait_recv()
            here = slice(part * lanes, (part + 1) * lanes)
            x = acc[c, 0:rows, here] + rs_recv[c, :, here].astype(F32)
            out_ref[:, pl.ds(pl.multiple_of(c * chunk + part * lanes, lanes), lanes)] = x
            sq_send[c, :, here] = jnp.sum(x * x, axis=0, keepdims=True)

        for i in range(2 * own_z):

            @pl.when(c * (2 * own_z) + i == me)
            def _():
                sq_recv[me] = sq_send[c]

            @pl.when(c * (2 * own_z) + i != me)
            def _():
                sq_copy(c, i).start()

    def share_out(c):
        y_copy(c).wait_recv()
        for i in range(own_z):
            total = pay[c, y, i] + y_recv[c, i]
            padded = jnp.concatenate([total, jnp.zeros((8, 128), F32)], axis=0).astype(BF16)
            z_send[c, i] = padded

            @pl.when(c * own_z + i == z)
            def _():
                z_recv[z] = padded

            @pl.when(c * own_z + i != z)
            def _():
                z_copy(c, i).start()

    @pl.loop(0, (n_chunks - 1) // PAIR + half + 3)
    def _(slot):
        @pl.loop(0, n_chunks)
        def _(c):
            step = slot - c // PAIR

            @pl.when(step == 0)
            def _():
                for part in range(parts):
                    attend(c, part)
                    ring_full(c, part, 1, 0).start()
                    ring_full(c, part, 1, 1).start()
                first = jnp.dot(wbuf[z], att[z, c], preferred_element_type=F32)
                columns = pl.ds(pl.multiple_of(c * chunk, chunk), chunk)
                acc[c, 0:rows] = first[0:rows] + hid_ref[:, columns].astype(F32)
                acc[c, rows : 2 * rows] = first[rows : 2 * rows]

            @pl.when(jnp.logical_and(step >= 1, step < half))
            def _():
                for part in range(parts):
                    for way in range(2):
                        ring_full(c, part, step, way).wait_recv()

                        @pl.when(step < half - 1)
                        def _():
                            ring_full(c, part, step + 1, way).start()

                        @pl.when(step == half - 1)
                        def _():
                            ring_half(c, part, step + 1, way).start()

                low = (z + n_z - step) % n_z
                high = (z + step) % n_z
                weights = jnp.concatenate([wbuf[low], wbuf[high]], axis=1)
                blocks = jnp.concatenate([att[low, c], att[high, c]], axis=0)
                acc[c] += jnp.dot(weights, blocks, preferred_element_type=F32)

            @pl.when(step == half)
            def _():
                far = (z + half) % n_z
                for part in range(parts):
                    ring_half(c, part, step, 0).wait_recv()
                    ring_half(c, part, step, 1).wait_recv()
                    here = slice(part * lanes, (part + 1) * lanes)
                    last = acc[c, :, here] + jnp.dot(wbuf[far], att[far, c, :, here], preferred_element_type=F32)
                    acc[c, :, here] = last
                    rs_send[c, :, here] = last[rows : 2 * rows].astype(BF16)
                    rs_copy(c, part).start()
                part_velocity(c)

            @pl.when(step == half + 1)
            def _():
                finish_block(c)

            @pl.when(step == half + 2)
            def _():
                share_out(c)

    whole(z_recv.at[pl.ds(0, n_z - 1)], z_rsem).wait()
    total = z_recv[0].astype(F32)
    for i in range(1, n_z):
        total = total + z_recv[i].astype(F32)
    total = total[0 : tok // 2]
    for i in range(2 * own_z):

        @pl.when(me % (2 * own_z) == i)
        def _():
            whole(sq_recv.at[pl.ds(0, n_seq - 1), :, lanes_of(i)], sq_rsem).wait()

    squares = jnp.sum(sq_recv[...], axis=0)
    sq_column[...] = jnp.broadcast_to(lax.rsqrt(squares / d_out + 1e-06), (128, chunk)).T
    scale = sq_column[pl.ds(pl.multiple_of(me % (2 * own_z) * tok, 8), tok), 0:64]
    velocity = jnp.concatenate([total[:, 0:64], total[:, 64:128]], axis=0) * scale
    vel_ref[...] = velocity
    level = jnp.full(velocity.shape, lev_ref[0].astype(F32), F32)
    delta = sigma_of(level + 1.0) - sigma_of(level)
    n_send[:, 0:64] = lat_ref[...] + delta * velocity
    n_send[:, 64:128] = jnp.zeros_like(velocity)
    onward = pltpu.make_async_remote_copy(
        src_ref=n_send, dst_ref=n_recv, send_sem=n_ssem, recv_sem=n_rsem, device_id=(after, me), device_id_type=MESH
    )
    onward.start()

    whole(qkv.at[pl.ds(1, 2), pl.ds(0, others)], kv_send).wait()
    whole(qkv.at[pl.ds(0, 1), pl.ds(0, others)], q_send).wait()
    whole(wbuf.at[:, pl.ds(rows, rows)], w_send).wait()
    hw_copy.wait_send()

    for way in range(2):
        whole(att.at[pl.ds(0, half - 1)], ag_send.at[way]).wait()
        whole(att.at[0, :, pl.ds(0, hd // 2)], ag_send.at[way]).wait()
    whole(rs_recv, rs_ssem).wait()
    whole(y_recv, y_ssem).wait()
    whole(z_recv.at[pl.ds(0, n_z - 1)], z_ssem).wait()
    for i in range(2 * own_z):

        @pl.when(me % (2 * own_z) != i)
        def _():
            whole(sq_recv.at[pl.ds(0, n_chunks), :, lanes_of(i)], sq_ssem).wait()

        @pl.when(me % (2 * own_z) == i)
        def _():
            whole(sq_recv.at[pl.ds(0, n_chunks - 1), :, lanes_of(i)], sq_ssem).wait()


    onward.wait()
    next_ref[...] = jnp.where(group == 0, fresh_ref[...], n_recv[:, 0:64])


def write_out(*refs):
    sems = refs[6]
    copies = [pltpu.make_async_copy(refs[i], refs[3 + i], sems.at[i]) for i in range(3)]
    for copy in copies:
        copy.start()
    for copy in copies:
        copy.wait()


def solution(mesh):
    n_queue, n_seq = mesh.shape["queue"], mesh.shape["seq"]
    n_z = n_seq // 2
    n_chunks = 4 if n_z >= 8 else 2

    def on_device(projected, out_weight, head_weight, hidden_in, latent, fresh_noise, levels):
        tok, width = projected.shape[1:]
        hd = width // n_seq
        rows, n_tok = hidden_in.shape
        chunk = n_tok // n_chunks
        own_z = n_z // n_chunks
        half = n_z // 2
        parts = chunk // math.gcd(chunk, 128)
        vmem = pl.BlockSpec(memory_space=pltpu.VMEM)
        hbm = pl.BlockSpec(memory_space=pltpu.HBM)
        dma = pltpu.SemaphoreType.DMA
        results = pl.pallas_call(
            functools.partial(kernel, n_queue, n_z, n_chunks, rows * n_seq),
            out_shape=(
                pltpu.VMEM((rows, n_tok), F32),
                pltpu.VMEM((tok, 64), F32),
                pltpu.VMEM((tok, 64), F32),
            ),
            in_specs=[hbm, hbm, hbm, hbm, hbm, hbm, pl.BlockSpec(memory_space=pltpu.SMEM)],
            out_specs=(vmem, vmem, vmem),
            scratch_shapes=[
                pltpu.VMEM((3, tok, width), BF16),
                pltpu.VMEM((3, n_tok, hd), BF16),
                pltpu.VMEM((hd, n_tok), BF16),
                pltpu.VMEM((n_tok, math.gcd(chunk, 128)), F32),
                pltpu.VMEM((n_z, n_chunks, hd, chunk), BF16),
                pltpu.VMEM((n_z, 2 * rows, hd), BF16),
                pltpu.VMEM((n_chunks, 2 * rows, chunk), F32),
                pltpu.VMEM((64, rows), BF16),
                pltpu.VMEM((rows, n_tok), BF16),
                pltpu.VMEM((tok, 64), F32),
                pltpu.VMEM((tok, 64), F32),
                pltpu.VMEM((2 * rows, 128), BF16),
                pltpu.VMEM((n_chunks, rows, chunk), BF16),
                pltpu.VMEM((n_chunks, rows, chunk), BF16),
                pltpu.VMEM((n_chunks, 1, chunk), F32),
                pltpu.VMEM((n_seq, 1, chunk), F32),
                pltpu.VMEM((chunk, 128), F32),
                pltpu.VMEM((n_chunks, 2, own_z, tok // 2, 128), F32),
                pltpu.VMEM((n_chunks, own_z, tok // 2, 128), F32),
                pltpu.VMEM((n_chunks, own_z, tok // 2 + 8, 128), BF16),
                pltpu.VMEM((n_z, tok // 2 + 8, 128), BF16),
                pltpu.VMEM((tok, 128), F32),
                pltpu.VMEM((tok, 128), F32),
                dma, dma((4,)), dma, dma, dma, dma, dma, dma, dma, dma, dma, dma,
                dma((2,)),
                dma((2, n_chunks, parts, 3)),
                dma,
                dma((n_chunks, parts)),
                dma,
                dma,
                dma,
                dma((n_chunks,)),
                dma,
                dma,
                dma,
                dma,
            ],
            compiler_params=pltpu.CompilerParams(
                collective_id=0, has_side_effects=True, vmem_limit_bytes=62 * 1024 * 1024
            ),
        )(projected, out_weight, head_weight.T, hidden_in, latent, fresh_noise, levels)
        return pl.pallas_call(
            write_out,
            out_shape=tuple(jax.ShapeDtypeStruct(r.shape, r.dtype) for r in results),
            in_specs=[vmem] * 3,
            out_specs=(hbm, hbm, hbm),
            scratch_shapes=[dma((3,))],
            compiler_params=pltpu.CompilerParams(vmem_limit_bytes=4 * 1024 * 1024),
        )(*results)

    return jax.shard_map(
        on_device,
        mesh=mesh,
        in_specs=(
            P(None, ("queue", "seq"), None),
            P("seq", None),
            P("seq", None),
            P("seq", "queue"),
            P(("queue", "seq"), None),
            P("seq", None),
            P("queue"),
        ),
        out_specs=(P("seq", "queue"), P(("queue", "seq"), None), P(("queue", "seq"), None)),
        check_vma=False,
    )
```
